128 devices in a mesh: front: 8 (over x, core), row: 16 (over z, y).
Axes of the slice: x: 4, y: 4, z: 4, core: 2. Of those that a mesh axis runs over, the one named last changes fastest.
Arguments:
- parent: bfloat16 [8192, 8192], P(('front', 'row')), as said below
- margin: int32 [16, 16], P('front'), may hold values from 0 to 63, as said below
- counts: int32 [16], P('front'), may hold values from 8 to 16, as said below
- factor: bfloat16 [16, 2048, 4096], P('front', None, 'row'), may hold values from -0.125 to 0.125
- local_inverse: bfloat16 [16, 4096, 4096], P('front', None, 'row'), may hold values from -0.09375 to 0.09375
Outputs:
- coupling: bfloat16 [16, 2048, 4096], P('front', None, 'row')
- diag_blocks: float32 [16, 32, 128, 128], P('front', 'row')
The draws below stay inside these ranges and needn't reach their ends.
Inputs may be any that keep to these rules, and one draw needn't show every extreme that they name: parent is exactly symmetric. The 16 entries of each row of margin are distinct. `counts`: some front has all 16 update blocks live.
All inputs are finite; a program needn't handle non-finite values.
Results may differ from the reference program's by a relative error of at most 0.0025.
Values may be sent and summed in bfloat16 or wider, within the bound.
A program may use at most 128 MiB of HBM per device.

```python
import jax
import jax.numpy as jnp
from jax import lax

K = 4096
BLOCK = 128
NOV = 16
NBP = 64
FRONTS = 16
PARENT = 8192
UPDATE = 2048


def draw_parent(key, part):
    base_draw = jax.random.normal(key, (PARENT, PARENT), jnp.float32)
    symmetric = (base_draw + base_draw.T) * 0.7071
    return symmetric.astype(jnp.bfloat16)


def draw_margin(key, part):
    front_keys = jax.random.split(key, FRONTS)
    return jax.vmap(lambda one_key: jax.random.permutation(one_key, NBP)[:NOV])(front_keys).astype(jnp.int32)


def draw_counts(key, part):
    values = jax.random.randint(key, (FRONTS,), NOV // 2, NOV + 1, jnp.int32)
    position = jax.random.randint(jax.random.fold_in(key, 5), (), 0, FRONTS, jnp.int32)
    return values.at[position].set(NOV)


def block_scale(own_key, dims, shards, least, largest):
    def one(axis_at, parts):
        draws = jax.random.uniform(jax.random.fold_in(jax.random.fold_in(own_key, 6), axis_at), (parts,), jnp.float32, least / len(shards), largest / len(shards))
        return jnp.repeat(jnp.exp(draws), dims[axis_at] // parts).reshape((-1,) + (1,) * (len(dims) - axis_at - 1))

    gain = one(*shards[0])
    for cut in shards[1:]:
        gain = gain * one(*cut)
    return gain


def gaussian(rng, shape, deviation, reach, shards=(), kind=jnp.bfloat16):
    drawn = deviation * jax.random.normal(rng, shape, jnp.float32)
    if shards:
        drawn = drawn * block_scale(rng, shape, shards, -0.22, 0.18)
    return jnp.clip(drawn, -reach, reach).astype(kind)


def setup_inputs(seed: int = 0) -> dict:
    keys = jax.random.split(jax.random.key(seed), 6)
    parent = draw_parent(jax.random.fold_in(keys[5], 71), 0)
    margin = draw_margin(jax.random.fold_in(keys[5], 71), 0)
    counts = draw_counts(jax.random.fold_in(keys[5], 71), 0)
    factor = gaussian(keys[3], (FRONTS, UPDATE, K), UPDATE ** -0.5, 0.125, ((0, 8), (2, 16)))
    local_inverse = gaussian(keys[4], (FRONTS, K, K), K ** -0.5, 0.09375, ((0, 8), (2, 16)))
    return {"parent": parent, "margin": margin, "counts": counts, "factor": factor, "local_inverse": local_inverse}


def reference(parent, margin, counts, factor, local_inverse):
    parent_grid = parent.reshape(NBP, BLOCK, NBP, BLOCK)
    block_of_row = jnp.arange(UPDATE, dtype=jnp.int32) // BLOCK
    lower_mask = jnp.arange(K, dtype=jnp.int32)[:, None] >= jnp.arange(K, dtype=jnp.int32)[None, :]

    def one_front(inputs):
        picked_blocks, live_count, front_factor, front_inverse = inputs
        sub_inverse = jnp.take(jnp.take(parent_grid, picked_blocks, axis=0), picked_blocks, axis=2).reshape(UPDATE, UPDATE)
        live_rows = block_of_row < live_count
        live_factor = jnp.where(live_rows[:, None], front_factor, jnp.zeros_like(front_factor))
        product = jnp.dot(sub_inverse, live_factor, preferred_element_type=jnp.float32)
        coupling = jnp.where(live_rows[:, None], -product, jnp.zeros_like(product)).astype(jnp.bfloat16)
        triangle = jnp.where(lower_mask, front_inverse, jnp.zeros_like(front_inverse)).astype(jnp.float32).reshape(K, K // BLOCK, BLOCK)
        local_term = jnp.einsum("kcx,kcy->cxy", triangle, triangle, precision=lax.Precision.HIGHEST)
        factor_blocks = live_factor.astype(jnp.float32).reshape(UPDATE, K // BLOCK, BLOCK)
        coupling_blocks = coupling.astype(jnp.float32).reshape(UPDATE, K // BLOCK, BLOCK)
        cross_term = jnp.einsum("rcx,rcy->cxy", factor_blocks, coupling_blocks, precision=lax.Precision.HIGHEST)
        return coupling, local_term - cross_term

    coupling, diag_blocks = lax.map(one_front, (margin, counts, factor, local_inverse))
    return coupling, diag_blocks
```

```python
import functools

import jax
import jax.numpy as jnp
from jax import lax
from jax.experimental import pallas as pl
from jax.experimental.pallas import tpu as pltpu
from jax.sharding import PartitionSpec as P

MESH = pl.DeviceIdType.MESH
NOV = 16
BLOCK = 128
BAND = 9
SLICES = 64


def place(x, core, y, z):
    return (2 * x + core, 4 * z + y)


def gather_kernel(
    parent_ref, margin_ref, out_ref,
    slabs, picked, margin_buf, margin_smem,
    t_send, t_recv, d_send, d_recv, m_send, m_recv, l_sem, x_send, x_recv, g_send, g_recv,
):
    front = lax.axis_index("front")
    row = lax.axis_index("row")
    x, core = front // 2, front % 2
    z, y = row // 4, row % 4
    half, yh = y % 2, y // 2
    me_q = yh * 16 + z * 4 + x
    my_block = 16 * x + 8 * core + 2 * z + yh
    my_slice = half * 32 + me_q
    sibling = place(x, 1 - core, y, z)
    y_up = place(x, core, (y + 1) % 4, z)
    y_down = place(x, core, (y + 3) % 4, z)
    z_up = place(x, core, y, (z + 1) % 4)
    z_down = place(x, core, y, (z + 3) % 4)

    def member(q):
        return place(q % 4, core, 2 * (q // 16) + half, (q // 4) % 4)

    barrier = pltpu.get_barrier_semaphore()

    def greet(step, _):
        pl.semaphore_signal(
            barrier, inc=1, device_id=member((me_q + step) % 32), device_id_type=MESH
        )
        return 0

    lax.fori_loop(1, 32, greet, 0)
    for other in (sibling, y_up, y_down):
        pl.semaphore_signal(barrier, inc=1, device_id=other, device_id_type=MESH)
    pl.semaphore_wait(barrier, 34)

    margin_sends = []
    for step in (1, 2, 3):
        copy = pltpu.make_async_remote_copy(
            src_ref=margin_ref,
            dst_ref=margin_buf.at[x],
            send_sem=m_send.at[step],
            recv_sem=m_recv.at[x],
            device_id=place((x + step) % 4, core, y, z),
            device_id_type=MESH,
        )
        copy.start()
        margin_sends.append(copy)
    own_margin = pltpu.make_async_copy(margin_ref, margin_buf.at[x], m_recv.at[x])
    own_margin.start()

    own_slab = pltpu.make_async_copy(
        parent_ref.at[me_q // 4, :, me_q % 4], slabs.at[my_block], t_recv.at[x]
    )
    own_slab.start()

    def spread(step, _):
        q = (me_q + step) % 32
        pltpu.make_async_remote_copy(
            src_ref=parent_ref.at[q // 4, :, q % 4],
            dst_ref=slabs.at[my_block],
            send_sem=t_send,
            recv_sem=t_recv.at[x],
            device_id=member(q),
            device_id_type=MESH,
        ).start()
        return 0

    lax.fori_loop(1, 32, spread, 0)

    for source in range(4):
        pltpu.make_async_copy(margin_ref, margin_buf.at[source], m_recv.at[source]).wait()
    to_smem = pltpu.make_async_copy(margin_buf, margin_smem, l_sem.at[0])
    to_smem.start()

    exchanges = []
    for source in range(4):
        group = slabs.at[pl.ds(16 * source + 8 * core, 8)]
        pltpu.make_async_copy(group, group, t_recv.at[source]).wait()
        copy = pltpu.make_async_remote_copy(
            src_ref=group,
            dst_ref=group,
            send_sem=d_send.at[source],
            recv_sem=d_recv.at[source],
            device_id=sibling,
            device_id_type=MESH,
        )
        copy.start()
        exchanges.append(copy)
    to_smem.wait()
    for copy in exchanges:
        copy.wait()

    x_copies = []
    for step in (2, 1, 3, 0):
        target = (x + step) % 4

        def pick(index, _):
            part, a = index // NOV, index % NOV
            block_row = margin_smem[target, part, a]
            for d in range(BAND):
                block_col = margin_smem[target, part, a + d]
                picked[target, part, a, d] = slabs[block_row, block_col]
            return 0

        lax.fori_loop(0, 2 * NOV, pick, 0)
        if step:
            copy = pltpu.make_async_remote_copy(
                src_ref=picked.at[target],
                dst_ref=out_ref.at[:, :, :, my_slice],
                send_sem=x_send.at[step],
                recv_sem=x_recv.at[4 - step],
                device_id=place(target, core, y, z),
                device_id_type=MESH,
            )
        else:
            copy = pltpu.make_async_copy(
                picked.at[target], out_ref.at[:, :, :, my_slice], l_sem.at[1]
            )
        copy.start()
        x_copies.append(copy)
    for copy in x_copies:
        copy.wait()

    def y_chunk(part, lo, size, y_at):
        first = (y_at % 2) * 32 + (y_at // 2) * 16 + z * 4
        return out_ref.at[part, pl.ds(lo, size), :, pl.ds(first, 4)]

    def z_slab(part, lo, size, z_at):
        return [
            out_ref.at[part, pl.ds(lo, size), :, pl.ds(o * 16 + z_at * 4, 4)] for o in range(4)
        ]

    def z_chunk(part, lo, size, z_at):
        first = half * 32 + yh * 16 + z_at * 4
        return out_ref.at[part, pl.ds(lo, size), :, pl.ds(first, 4)]

    def y_slab(part, lo, size, y_at):
        first = (y_at % 2) * 32 + (y_at // 2) * 16
        return out_ref.at[part, pl.ds(lo, size), :, pl.ds(first, 16)]

    def send(ref, slot, device):
        copy = pltpu.make_async_remote_copy(
            src_ref=ref, dst_ref=ref, send_sem=g_send.at[slot], recv_sem=g_recv.at[slot],
            device_id=device, device_id_type=MESH,
        )
        copy.start()
        return copy

    def landed(ref, slot):
        pltpu.make_async_copy(ref, ref, g_recv.at[slot]).wait()

    up_y, down_y = (y + 1) % 4, (y + 3) % 4
    up_z, down_z = (z + 1) % 4, (z + 3) % 4
    sends = []
    sends.append(send(y_chunk(0, 0, NOV, y), 0, y_up))
    sends.append(send(z_chunk(1, 0, NOV, z), 1, z_up))
    sends.append(send(y_chunk(0, 0, NOV, y), 2, y_down))
    sends.append(send(z_chunk(1, 0, NOV, z), 3, z_down))
    landed(y_chunk(0, 0, NOV, down_y), 0)
    sends.append(send(y_chunk(0, 0, 8, down_y), 4, y_up))
    landed(z_chunk(1, 0, NOV, down_z), 1)
    sends.append(send(z_chunk(1, 0, 8, down_z), 5, z_up))
    landed(y_chunk(0, 0, NOV, up_y), 2)
    sends.append(send(y_chunk(0, 8, 8, up_y), 6, y_down))
    landed(z_chunk(1, 0, NOV, up_z), 3)
    sends.append(send(z_chunk(1, 8, 8, up_z), 7, z_down))
    far_y, far_z = (y + 2) % 4, (z + 2) % 4
    landed(y_chunk(0, 0, 8, far_y), 4)
    landed(y_chunk(0, 8, 8, far_y), 6)
    landed(z_chunk(1, 0, 8, far_z), 5)
    landed(z_chunk(1, 8, 8, far_z), 7)

    def send_slab(pieces, slot, device):
        for o, piece in enumerate(pieces):
            sends.append(send(piece, slot + o, device))

    def slab_landed(pieces, slot):
        for o, piece in enumerate(pieces):
            landed(piece, slot + o)

    send_slab(z_slab(0, 0, NOV, z), 8, z_up)
    sends.append(send(y_slab(1, 0, NOV, y), 24, y_up))
    send_slab(z_slab(0, 0, NOV, z), 12, z_down)
    sends.append(send(y_slab(1, 0, NOV, y), 25, y_down))
    slab_landed(z_slab(0, 0, NOV, down_z), 8)
    send_slab(z_slab(0, 0, 8, down_z), 16, z_up)
    landed(y_slab(1, 0, NOV, down_y), 24)
    sends.append(send(y_slab(1, 0, 8, down_y), 26, y_up))
    slab_landed(z_slab(0, 0, NOV, up_z), 12)
    send_slab(z_slab(0, 8, 8, up_z), 20, z_down)
    landed(y_slab(1, 0, NOV, up_y), 25)
    sends.append(send(y_slab(1, 8, 8, up_y), 27, y_down))
    slab_landed(z_slab(0, 0, 8, far_z), 16)
    slab_landed(z_slab(0, 8, 8, far_z), 20)
    landed(y_slab(1, 0, 8, far_y), 26)
    landed(y_slab(1, 8, 8, far_y), 27)

    for copy in sends:
        copy.wait_send()
    for copy in margin_sends:
        copy.wait_send()
    sent = slabs.at[pl.ds(0, 31)]
    pltpu.make_async_copy(sent, sent, t_send).wait()


def gathered(parent, margin):
    grid = parent.reshape(8, 4, 2, 64, BLOCK).transpose(0, 3, 1, 2, 4)
    wide = jnp.concatenate([margin, margin], axis=1)
    wide = jnp.pad(wide, ((0, 6), (0, 128 - 2 * NOV)))
    dma = pltpu.SemaphoreType.DMA
    return pl.pallas_call(
        gather_kernel,
        out_shape=jax.ShapeDtypeStruct((2, NOV, BAND, SLICES, 2, BLOCK), jnp.bfloat16),
        in_specs=[pl.BlockSpec(memory_space=pl.ANY), pl.BlockSpec(memory_space=pltpu.VMEM)],
        out_specs=pl.BlockSpec(memory_space=pltpu.VMEM),
        scratch_shapes=[
            pltpu.VMEM((64, 64, 2, BLOCK), jnp.bfloat16),
            pltpu.VMEM((4, 2, NOV, BAND, 2, BLOCK), jnp.bfloat16),
            pltpu.VMEM((4, 8, 128), jnp.int32),
            pltpu.SMEM((4, 8, 128), jnp.int32),
            dma, dma((4,)), dma((4,)), dma((4,)), dma((4,)), dma((4,)), dma((2,)),
            dma((4,)), dma((4,)), dma((28,)), dma((28,)),
        ],
        compiler_params=pltpu.CompilerParams(
            collective_id=0, has_side_effects=True, vmem_limit_bytes=40 * 2**20
        ),
        cost_estimate=pl.CostEstimate(flops=0, bytes_accessed=10 * 2**20, transcendentals=0),
    )(grid, wide)


def update_kernel(counts_ref, sub_ref, factor_ref, inverse_ref, coupling_ref, diag_ref, live):
    count = counts_ref[pl.program_id(0)]
    first_col = lax.axis_index("row") * 256

    def mask(a, _):
        rows = pl.multiple_of(a * BLOCK, BLOCK)
        value = factor_ref[0, pl.ds(rows, BLOCK), :]
        value = jnp.where(a < count, value, jnp.zeros_like(value))
        live[pl.ds(rows, BLOCK), :] = value
        live[pl.ds(rows + NOV * BLOCK, BLOCK), :] = value
        return 0

    lax.fori_loop(0, NOV, mask, 0)

    def block_row(a, _):
        rows = pl.multiple_of(a * BLOCK, BLOCK)
        direct = jnp.concatenate([sub_ref[0, a, d] for d in range(BAND)], axis=1)
        total = jnp.dot(
            direct, live[pl.ds(rows, BAND * BLOCK), :], preferred_element_type=jnp.float32
        )
        mirrored = jnp.concatenate(
            [sub_ref[0, (a + NOV - d) % NOV, d] for d in range(7, 0, -1)], axis=0
        )
        total += lax.dot_general(
            mirrored, live[pl.ds(rows + 9 * BLOCK, 7 * BLOCK), :],
            (((0,), (0,)), ((), ())), preferred_element_type=jnp.float32,
        )
        total = jnp.where(a < count, -total, jnp.zeros_like(total))
        coupling_ref[0, pl.ds(rows, BLOCK), :] = total.astype(jnp.bfloat16)
        return 0

    lax.fori_loop(0, NOV, block_row, 0)

    def local(step, total):
        rows = pl.multiple_of(step * 512, 512)
        value = inverse_ref[0, pl.ds(rows, 512), :]
        row_at = rows + lax.broadcasted_iota(jnp.int32, value.shape, 0)
        col_at = first_col + lax.broadcasted_iota(jnp.int32, value.shape, 1)
        value = jnp.where(row_at >= col_at, value, jnp.zeros_like(value))
        return total + lax.dot_general(
            value, value, (((0,), (0,)), ((), ())), preferred_element_type=jnp.float32
        )

    total = lax.fori_loop(0, 8, local, jnp.zeros((256, 256), jnp.float32))

    def cross(step, total):
        rows = pl.multiple_of(step * 512, 512)
        return total - lax.dot_general(
            live[pl.ds(rows, 512), :], coupling_ref[0, pl.ds(rows, 512), :],
            (((0,), (0,)), ((), ())), preferred_element_type=jnp.float32,
        )

    total = lax.fori_loop(0, 4, cross, total)
    for c in range(2):
        at = slice(c * BLOCK, (c + 1) * BLOCK)
        diag_ref[0, c] = total[at, at]


def body(parent, margin, counts, factor, local_inverse):
    sub = gathered(parent, margin).reshape(2, NOV, BAND, BLOCK, BLOCK)
    return pl.pallas_call(
        update_kernel,
        grid=(2,),
        out_shape=(
            jax.ShapeDtypeStruct(factor.shape, jnp.bfloat16),
            jax.ShapeDtypeStruct((2, 2, BLOCK, BLOCK), jnp.float32),
        ),
        in_specs=[
            pl.BlockSpec(memory_space=pltpu.SMEM),
            pl.BlockSpec((1, NOV, BAND, BLOCK, BLOCK), lambda f: (f, 0, 0, 0, 0)),
            pl.BlockSpec((1, 2048, 256), lambda f: (f, 0, 0)),
            pl.BlockSpec((1, 4096, 256), lambda f: (f, 0, 0)),
        ],
        out_specs=(
            pl.BlockSpec((1, 2048, 256), lambda f: (f, 0, 0)),
            pl.BlockSpec((1, 2, BLOCK, BLOCK), lambda f: (f, 0, 0, 0)),
        ),
        scratch_shapes=[pltpu.VMEM((4096, 256), jnp.bfloat16)],
        compiler_params=pltpu.CompilerParams(vmem_limit_bytes=40 * 2**20),
        cost_estimate=pl.CostEstimate(
            flops=6 * 10**9, bytes_accessed=20 * 2**20, transcendentals=0
        ),
    )(counts, sub, factor, local_inverse)


def solution(mesh):
    placed = (
        P(("front", "row"), None),
        P("front", None),
        P("front"),
        P("front", None, "row"),
        P("front", None, "row"),
    )
    return jax.shard_map(
        body,
        mesh=mesh,
        in_specs=placed,
        out_specs=(P("front", None, "row"), P("front", "row", None, None)),
        check_vma=False,
    )
```

```python
import functools

import jax
import jax.numpy as jnp
from jax import lax
from jax.experimental import pallas as pl
from jax.experimental.pallas import tpu as pltpu
from jax.sharding import PartitionSpec as P

MESH = pl.DeviceIdType.MESH
NOV = 16
BLOCK = 128
CHUNKS = 4
ROWS = NOV // CHUNKS


def place(x, core, y, z):
    return (2 * x + core, 4 * z + y)


def band(chunk):
    return 9 if chunk < CHUNKS // 2 else 8


def prepare(count, part, first_col, factor_buf, inverse_buf, live_ref, flipped_ref, local_ref):
    def mask(a, _):
        rows = pl.multiple_of(a * BLOCK, BLOCK)
        value = factor_buf[part, pl.ds(rows, BLOCK), :]
        value = jnp.where(a < count, value, jnp.zeros_like(value))
        turned = value.T
        for lap in range(2):
            at = pl.multiple_of(rows + lap * NOV * BLOCK, BLOCK)
            live_ref[part, pl.ds(at, BLOCK), :] = value
            flipped_ref[part, :, pl.ds(at, BLOCK)] = turned
        return 0

    lax.fori_loop(0, NOV, mask, 0)

    def local(step, total):
        rows = pl.multiple_of(step * 512, 512)
        value = inverse_buf[part, pl.ds(rows, 512), :]
        row_at = rows + lax.broadcasted_iota(jnp.int32, value.shape, 0)
        col_at = first_col + lax.broadcasted_iota(jnp.int32, value.shape, 1)
        value = jnp.where(row_at >= col_at, value, jnp.zeros_like(value))
        return total + lax.dot_general(
            value, value, (((0,), (0,)), ((), ())), preferred_element_type=jnp.float32
        )

    local_ref[part] = lax.fori_loop(0, 8, local, jnp.zeros((256, 256), jnp.float32))


def gather_kernel(
    counts_ref, parent_ref, margin_ref, factor_ref, inverse_ref,
    out_ref, live_ref, flipped_ref, local_ref,
    parent_buf, factor_buf, inverse_buf, slabs, picked, margin_buf, margin_smem,
    t_send, t_recv, d_send, d_recv, m_send, m_recv, l_sem, x_send, x_recv, g_send, g_recv,
):
    front = lax.axis_index("front")
    row = lax.axis_index("row")
    x, core = front // 2, front % 2
    z, y = row // 4, row % 4
    half, yh = y % 2, y // 2
    fold = half * 2 + yh
    me_q = yh * 16 + z * 4 + x
    my_block = 16 * x + 8 * core + 2 * z + yh
    sibling = place(x, 1 - core, y, z)
    y_up = place(x, core, (y + 1) % 4, z)
    y_down = place(x, core, (y + 3) % 4, z)
    z_up = place(x, core, y, (z + 1) % 4)
    z_down = place(x, core, y, (z + 3) % 4)

    def member(q):
        return place(q % 4, core, 2 * (q // 16) + half, (q // 4) % 4)

    parent_load = pltpu.make_async_copy(parent_ref, parent_buf, l_sem.at[0])
    parent_load.start()
    factor_load = pltpu.make_async_copy(factor_ref, factor_buf, l_sem.at[1])
    factor_load.start()
    inverse_load = pltpu.make_async_copy(inverse_ref, inverse_buf, l_sem.at[2])
    inverse_load.start()

    barrier = pltpu.get_barrier_semaphore()

    def greet(step, _):
        pl.semaphore_signal(
            barrier, inc=1, device_id=member((me_q + step) % 32), device_id_type=MESH
        )
        return 0

    lax.fori_loop(1, 32, greet, 0)
    for other in (sibling, y_up, y_down):
        pl.semaphore_signal(barrier, inc=1, device_id=other, device_id_type=MESH)
    parent_load.wait()
    pl.semaphore_wait(barrier, 34)

    margin_sends = []
    for step in (1, 2, 3):
        copy = pltpu.make_async_remote_copy(
            src_ref=margin_ref,
            dst_ref=margin_buf.at[x],
            send_sem=m_send.at[step],
            recv_sem=m_recv.at[x],
            device_id=place((x + step) % 4, core, y, z),
            device_id_type=MESH,
        )
        copy.start()
        margin_sends.append(copy)
    pltpu.make_async_copy(margin_ref, margin_buf.at[x], m_recv.at[x]).start()
    pltpu.make_async_copy(
        parent_buf.at[me_q // 4, :, me_q % 4], slabs.at[my_block], t_recv.at[x]
    ).start()

    def spread(step, _):
        q = (me_q + step) % 32
        pltpu.make_async_remote_copy(
            src_ref=parent_buf.at[q // 4, :, q % 4],
            dst_ref=slabs.at[my_block],
            send_sem=t_send,
            recv_sem=t_recv.at[x],
            device_id=member(q),
            device_id_type=MESH,
        ).start()
        return 0

    lax.fori_loop(1, 32, spread, 0)

    for source in range(4):
        pltpu.make_async_copy(margin_ref, margin_buf.at[source], m_recv.at[source]).wait()
    to_smem = pltpu.make_async_copy(margin_buf, margin_smem, l_sem.at[3])
    to_smem.start()
    to_smem.wait()

    factor_load.wait()
    inverse_load.wait()
    for part in range(2):
        prepare(
            counts_ref[part], part, row * 256, factor_buf, inverse_buf,
            live_ref, flipped_ref, local_ref,
        )

    exchanges = []
    for source in range(4):
        group = slabs.at[pl.ds(16 * source + 8 * core, 8)]
        pltpu.make_async_copy(group, group, t_recv.at[source]).wait()
        copy = pltpu.make_async_remote_copy(
            src_ref=group,
            dst_ref=group,
            send_sem=d_send.at[source],
            recv_sem=d_recv.at[source],
            device_id=sibling,
            device_id_type=MESH,
        )
        copy.start()
        exchanges.append(copy)
    for copy in exchanges:
        copy.wait()

    def x_part(ref, chunk):
        return ref.at[:, pl.ds(chunk * ROWS, ROWS), pl.ds(0, band(chunk))]

    def landing(chunk):
        return out_ref.at[
            :, pl.ds(chunk * ROWS, ROWS), pl.ds(0, band(chunk)), fold, z, x
        ]

    x_copies = [[] for _ in range(CHUNKS)]
    for chunk in range(CHUNKS):
        for step in (2, 1, 3, 0):
            target = (x + step) % 4

            def pick(index, _):
                part, a = index // ROWS, chunk * ROWS + index % ROWS
                block_row = margin_smem[target, part, a]
                for d in range(band(chunk)):
                    block_col = margin_smem[target, part, (a + d) % NOV]
                    picked[target, part, a, d] = slabs[block_row, block_col]
                return 0

            lax.fori_loop(0, 2 * ROWS, pick, 0)
            slot = 4 * chunk + step
            if step:
                copy = pltpu.make_async_remote_copy(
                    src_ref=x_part(picked.at[target], chunk),
                    dst_ref=landing(chunk),
                    send_sem=x_send.at[slot],
                    recv_sem=x_recv.at[slot],
                    device_id=place(target, core, y, z),
                    device_id_type=MESH,
                )
            else:
                copy = pltpu.make_async_copy(
                    x_part(picked.at[target], chunk), landing(chunk), x_recv.at[slot]
                )
            copy.start()
            x_copies[chunk].append(copy)

    def first_piece(part, lo, size, chunk, at):
        rows, dists = pl.ds(lo, size), pl.ds(0, band(chunk))
        if part == 0:
            return out_ref.at[0, rows, dists, (at % 2) * 2 + at // 2, z]
        return out_ref.at[1, rows, dists, fold, at]

    def second_piece(part, lo, size, chunk, at):
        rows, dists = pl.ds(lo, size), pl.ds(0, band(chunk))
        if part == 0:
            return out_ref.at[0, rows, dists, :, at]
        return out_ref.at[1, rows, dists, (at % 2) * 2 + at // 2]

    sends = []

    def send(ref, slot, device):
        copy = pltpu.make_async_remote_copy(
            src_ref=ref, dst_ref=ref, send_sem=g_send.at[slot], recv_sem=g_recv.at[slot],
            device_id=device, device_id_type=MESH,
        )
        copy.start()
        sends.append(copy)

    def landed(ref, slot):
        pltpu.make_async_copy(ref, ref, g_recv.at[slot]).wait()

    def ring(part, phase):
        if part == phase:
            return y, y_up, y_down
        return z, z_up, z_down

    def base(part, phase, chunk):
        return 4 * (part + 2 * (phase + 2 * chunk))

    pieces = (first_piece, second_piece)
    mid = ROWS // 2

    def start_direct(phase, chunk):
        for part in range(2):
            here, up, down = ring(part, phase)
            own = pieces[phase](part, chunk * ROWS, ROWS, chunk, here)
            send(own, base(part, phase, chunk), up)
            send(own, base(part, phase, chunk) + 1, down)

    def forward(phase, chunk):
        for part in range(2):
            here, up, down = ring(part, phase)
            slot, lo = base(part, phase, chunk), chunk * ROWS
            below, above = (here + 3) % 4, (here + 1) % 4
            landed(pieces[phase](part, lo, ROWS, chunk, below), slot)
            send(pieces[phase](part, lo, mid, chunk, below), slot + 2, up)
            landed(pieces[phase](part, lo, ROWS, chunk, above), slot + 1)
            send(pieces[phase](part, lo + mid, ROWS - mid, chunk, above), slot + 3, down)

    def finish(phase, chunk):
        for part in range(2):
            here = ring(part, phase)[0]
            slot, lo, far = base(part, phase, chunk), chunk * ROWS, (here + 2) % 4
            landed(pieces[phase](part, lo, mid, chunk, far), slot + 2)
            landed(pieces[phase](part, lo + mid, ROWS - mid, chunk, far), slot + 3)

    for turn in range(CHUNKS + 4):
        if turn < CHUNKS:
            for copy in x_copies[turn]:
                copy.wait()
            start_direct(0, turn)
        if 0 <= turn - 1 < CHUNKS:
            forward(0, turn - 1)
        if 0 <= turn - 2 < CHUNKS:
            finish(0, turn - 2)
            start_direct(1, turn - 2)
        if 0 <= turn - 3 < CHUNKS:
            forward(1, turn - 3)
        if 0 <= turn - 4 < CHUNKS:
            finish(1, turn - 4)

    for copy in sends:
        copy.wait_send()
    for copy in margin_sends:
        copy.wait_send()
    sent = slabs.at[pl.ds(0, 31)]
    pltpu.make_async_copy(sent, sent, t_send).wait()


def gathered(parent, margin, counts, factor, local_inverse):
    grid = parent.reshape(8, 4, 2, 64, BLOCK).transpose(0, 3, 1, 2, 4)
    dma = pltpu.SemaphoreType.DMA
    vmem = pl.BlockSpec(memory_space=pltpu.VMEM)
    hbm = pl.BlockSpec(memory_space=pltpu.HBM)
    return pl.pallas_call(
        gather_kernel,
        out_shape=(
            jax.ShapeDtypeStruct((2, NOV, 9, 4, 4, 4, 2, BLOCK), jnp.bfloat16),
            jax.ShapeDtypeStruct((2, 4096, 256), jnp.bfloat16),
            jax.ShapeDtypeStruct((2, 256, 4096), jnp.bfloat16),
            jax.ShapeDtypeStruct((2, 256, 256), jnp.float32),
        ),
        in_specs=[pl.BlockSpec(memory_space=pltpu.SMEM), hbm, vmem, hbm, hbm],
        out_specs=(vmem,) * 4,
        scratch_shapes=[
            pltpu.VMEM(grid.shape, jnp.bfloat16),
            pltpu.VMEM(factor.shape, jnp.bfloat16),
            pltpu.VMEM(local_inverse.shape, jnp.bfloat16),
            pltpu.VMEM((64, 64, 2, BLOCK), jnp.bfloat16),
            pltpu.VMEM((4, 2, NOV, 9, 2, BLOCK), jnp.bfloat16),
            pltpu.VMEM((4, 2, NOV), jnp.int32),
            pltpu.SMEM((4, 2, NOV), jnp.int32),
            dma, dma((4,)), dma((4,)), dma((4,)), dma((4,)), dma((4,)), dma((4,)),
            dma((4 * CHUNKS,)), dma((4 * CHUNKS,)), dma((16 * CHUNKS,)), dma((16 * CHUNKS,)),
        ],
        compiler_params=pltpu.CompilerParams(
            collective_id=0, has_side_effects=True, vmem_limit_bytes=28 * 2**20
        ),
        cost_estimate=pl.CostEstimate(
            flops=2 * 10**9, bytes_accessed=20 * 2**20, transcendentals=0
        ),
    )(counts, grid, margin, factor, local_inverse)


def update_kernel(counts_ref, sub_ref, live_ref, flipped_ref, local_ref, coupling_ref, diag_ref):
    part = pl.program_id(0)
    count = counts_ref[part]

    def pair(index, total, late):
        a = 2 * index
        rows = pl.multiple_of(a * BLOCK, 2 * BLOCK)
        zero = jnp.zeros((BLOCK, BLOCK), jnp.bfloat16)
        wide = 8 if late else 9
        deep = 8 if late else 7

        def block(r, d):
            return sub_ref[part, (r + NOV) % NOV, d]

        direct = jnp.concatenate(
            [
                jnp.concatenate([block(a, d) for d in range(wide)] + [zero], axis=1),
                jnp.concatenate([zero] + [block(a + 1, d) for d in range(wide)], axis=1),
            ],
            axis=0,
        )
        result = jnp.dot(
            direct, live_ref[part, pl.ds(rows, (wide + 1) * BLOCK), :],
            preferred_element_type=jnp.float32,
        )
        mirrored = jnp.concatenate(
            [
                jnp.concatenate([block(a - d, d), block(a - d, d + 1) if d < deep else zero], axis=1)
                if d
                else jnp.concatenate([zero, block(a, 1)], axis=1)
                for d in range(deep, -1, -1)
            ],
            axis=0,
        )
        start = pl.multiple_of(rows + (NOV - deep) * BLOCK, BLOCK)
        turned = jnp.dot(
            flipped_ref[part, :, pl.ds(start, (deep + 1) * BLOCK)], mirrored,
            preferred_element_type=jnp.float32,
        )
        result = -(result + turned.T)
        block_at = a + lax.broadcasted_iota(jnp.int32, result.shape, 0) // BLOCK
        result = jnp.where(block_at < count, result, jnp.zeros_like(result)).astype(jnp.bfloat16)
        coupling_ref[0, pl.ds(rows, 2 * BLOCK), :] = result
        return total - jnp.dot(
            flipped_ref[part, :, pl.ds(rows, 2 * BLOCK)], result,
            preferred_element_type=jnp.float32,
        )

    total = local_ref[part]
    total = lax.fori_loop(0, 4, functools.partial(pair, late=False), total)
    total = lax.fori_loop(4, 8, functools.partial(pair, late=True), total)
    for c in range(2):
        at = slice(c * BLOCK, (c + 1) * BLOCK)
        diag_ref[0, c] = total[at, at]


def body(parent, margin, counts, factor, local_inverse):
    sub, live, flipped, local = gathered(parent, margin, counts, factor, local_inverse)
    vmem = pl.BlockSpec(memory_space=pltpu.VMEM)
    return pl.pallas_call(
        update_kernel,
        grid=(2,),
        out_shape=(
            jax.ShapeDtypeStruct(factor.shape, jnp.bfloat16),
            jax.ShapeDtypeStruct((2, 2, BLOCK, BLOCK), jnp.float32),
        ),
        in_specs=[pl.BlockSpec(memory_space=pltpu.SMEM), vmem, vmem, vmem, vmem],
        out_specs=(
            pl.BlockSpec((1, 2048, 256), lambda f: (f, 0, 0)),
            pl.BlockSpec((1, 2, BLOCK, BLOCK), lambda f: (f, 0, 0, 0)),
        ),
        compiler_params=pltpu.CompilerParams(vmem_limit_bytes=16 * 2**20),
        cost_estimate=pl.CostEstimate(
            flops=6 * 10**9, bytes_accessed=20 * 2**20, transcendentals=0
        ),
    )(counts, sub.reshape(2, NOV, 9, BLOCK, BLOCK), live, flipped, local)


def solution(mesh):
    placed = (
        P(("front", "row"), None),
        P("front", None),
        P("front"),
        P("front", None, "row"),
        P("front", None, "row"),
    )
    return jax.shard_map(
        body,
        mesh=mesh,
        in_specs=placed,
        out_specs=(P("front", None, "row"), P("front", "row", None, None)),
        check_vma=False,
    )
```

```python
import functools

import jax
import jax.numpy as jnp
from jax import lax
from jax.experimental import pallas as pl
from jax.experimental.pallas import tpu as pltpu
from jax.sharding import PartitionSpec as P

MESH = pl.DeviceIdType.MESH
NOV = 16
BLOCK = 128
CHUNKS = 4
SLOTS = 20
ROWS = NOV // CHUNKS


def place(x, core, y, z):
    return (2 * x + core, 4 * z + y)


def band(chunk):
    return 9 if chunk < CHUNKS // 2 else 8


def prepare(count, part, first_col, factor_buf, inverse_buf, live_ref, flipped_ref, local_ref):
    def mask(a, _):
        rows = pl.multiple_of(a * BLOCK, BLOCK)
        value = factor_buf[part, pl.ds(rows, BLOCK), :]
        value = jnp.where(a < count, value, jnp.zeros_like(value))
        turned = value.T
        for lap in range(2):
            at = pl.multiple_of(rows + lap * NOV * BLOCK, BLOCK)
            live_ref[part, pl.ds(at, BLOCK), :] = value
            flipped_ref[part, :, pl.ds(at, BLOCK)] = turned
        return 0

    lax.fori_loop(0, NOV, mask, 0)

    def local(step, total):
        rows = pl.multiple_of(step * 512, 512)
        value = inverse_buf[part, pl.ds(rows, 512), :]
        row_at = rows + lax.broadcasted_iota(jnp.int32, value.shape, 0)
        col_at = first_col + lax.broadcasted_iota(jnp.int32, value.shape, 1)
        value = jnp.where(row_at >= col_at, value, jnp.zeros_like(value))
        return total + lax.dot_general(
            value, value, (((0,), (0,)), ((), ())), preferred_element_type=jnp.float32
        )

    local_ref[part] = lax.fori_loop(0, 8, local, jnp.zeros((256, 256), jnp.float32))


def gather_kernel(
    counts_ref, parent_ref, margin_ref, factor_ref, inverse_ref,
    out_ref, live_ref, flipped_ref, local_ref,
    parent_buf, factor_buf, inverse_buf, slabs, picked, margin_buf, margin_smem, counts_smem,
    t_send, t_recv, d_send, d_recv, m_send, m_recv, l_sem, x_send, x_recv, g_send, g_recv,
):
    front = lax.axis_index("front")
    row = lax.axis_index("row")
    x, core = front // 2, front % 2
    z, y = row // 4, row % 4
    half, yh = y % 2, y // 2
    fold = half * 2 + yh
    me_q = yh * 16 + z * 4 + x
    my_block = 16 * x + 8 * core + 2 * z + yh
    sibling = place(x, 1 - core, y, z)
    y_up = place(x, core, (y + 1) % 4, z)
    y_down = place(x, core, (y + 3) % 4, z)
    z_up = place(x, core, y, (z + 1) % 4)
    z_down = place(x, core, y, (z + 3) % 4)

    def member(q):
        return place(q % 4, core, 2 * (q // 16) + half, (q // 4) % 4)

    parent_load = pltpu.make_async_copy(parent_ref, parent_buf, l_sem.at[0])
    parent_load.start()
    factor_load = pltpu.make_async_copy(factor_ref, factor_buf, l_sem.at[1])
    factor_load.start()
    inverse_load = pltpu.make_async_copy(inverse_ref, inverse_buf, l_sem.at[2])
    inverse_load.start()
    counts_load = pltpu.make_async_copy(counts_ref, counts_smem, l_sem.at[4])
    counts_load.start()

    barrier = pltpu.get_barrier_semaphore()

    def greet(step, _):
        pl.semaphore_signal(
            barrier, inc=1, device_id=member((me_q + step) % 32), device_id_type=MESH
        )
        return 0

    lax.fori_loop(1, 32, greet, 0)
    for other in (sibling, y_up, y_down):
        pl.semaphore_signal(barrier, inc=1, device_id=other, device_id_type=MESH)
    parent_load.wait()
    pl.semaphore_wait(barrier, 34)

    margin_sends = []
    for step in (1, 2, 3):
        copy = pltpu.make_async_remote_copy(
            src_ref=margin_ref,
            dst_ref=margin_buf.at[x],
            send_sem=m_send.at[step],
            recv_sem=m_recv.at[x],
            device_id=place((x + step) % 4, core, y, z),
            device_id_type=MESH,
        )
        copy.start()
        margin_sends.append(copy)
    pltpu.make_async_copy(margin_ref, margin_buf.at[x], m_recv.at[x]).start()
    pltpu.make_async_copy(
        parent_buf.at[me_q // 4, :, me_q % 4], slabs.at[my_block], t_recv.at[x]
    ).start()

    for offset in (0, 1, 3, 2):

        def spread(step, _):
            q = (yh * 4 + z + step) % 8 * 4 + (x + offset) % 4
            pltpu.make_async_remote_copy(
                src_ref=parent_buf.at[q // 4, :, q % 4],
                dst_ref=slabs.at[my_block],
                send_sem=t_send,
                recv_sem=t_recv.at[x],
                device_id=member(q),
                device_id_type=MESH,
            ).start()
            return 0

        lax.fori_loop(0 if offset else 1, 8, spread, 0)

    for source in range(4):
        pltpu.make_async_copy(margin_ref, margin_buf.at[source], m_recv.at[source]).wait()
    to_smem = pltpu.make_async_copy(margin_buf, margin_smem, l_sem.at[3])
    to_smem.start()
    to_smem.wait()

    factor_load.wait()
    inverse_load.wait()
    counts_load.wait()
    for part in range(2):
        prepare(
            counts_smem[part], part, row * 256, factor_buf, inverse_buf,
            live_ref, flipped_ref, local_ref,
        )

    exchanges = []
    for offset in (0, 1, 3, 2):
        source = (x + 4 - offset) % 4
        group = slabs.at[pl.ds(16 * source + 8 * core, 8)]
        pltpu.make_async_copy(group, group, t_recv.at[source]).wait()
        copy = pltpu.make_async_remote_copy(
            src_ref=group,
            dst_ref=group,
            send_sem=d_send.at[source],
            recv_sem=d_recv.at[source],
            device_id=sibling,
            device_id_type=MESH,
        )
        copy.start()
        exchanges.append(copy)
    for copy in exchanges:
        copy.wait()

    def x_part(ref, chunk):
        return ref.at[:, pl.ds(chunk * ROWS, ROWS), pl.ds(0, band(chunk))]

    def landing(chunk):
        return out_ref.at[
            :, pl.ds(chunk * ROWS, ROWS), pl.ds(0, band(chunk)), fold, z, x
        ]

    x_copies = [[] for _ in range(CHUNKS)]

    def start_x(chunk):
        for step in (2, 1, 3, 0):
            target = (x + step) % 4

            def pick(index, _):
                part, a = index // ROWS, chunk * ROWS + index % ROWS
                block_row = margin_smem[target, part, a]
                for d in range(band(chunk)):
                    block_col = margin_smem[target, part, (a + d) % NOV]
                    picked[target, part, a, d] = slabs[block_row, block_col]
                return 0

            lax.fori_loop(0, 2 * ROWS, pick, 0)
            slot = 4 * chunk + step
            if step:
                copy = pltpu.make_async_remote_copy(
                    src_ref=x_part(picked.at[target], chunk),
                    dst_ref=landing(chunk),
                    send_sem=x_send.at[slot],
                    recv_sem=x_recv.at[slot],
                    device_id=place(target, core, y, z),
                    device_id_type=MESH,
                )
            else:
                copy = pltpu.make_async_copy(
                    x_part(picked.at[target], chunk), landing(chunk), x_recv.at[slot]
                )
            copy.start()
            x_copies[chunk].append(copy)

    first_axis = ((y, y_up, y_down), (z, z_up, z_down))
    sends = []

    def piece(part, chunk, first_at, second_at, lo=0, size=ROWS):
        y_at, z_at = (first_at, second_at) if part == 0 else (second_at, first_at)
        return out_ref.at[
            part, pl.ds(chunk * ROWS + lo, size), pl.ds(0, band(chunk)),
            (y_at % 2) * 2 + y_at // 2, z_at,
        ]

    def sem_at(part, chunk, slot):
        return SLOTS * (part + 2 * chunk) + slot

    def send(part, chunk, slot, ref, device):
        at = sem_at(part, chunk, slot)
        copy = pltpu.make_async_remote_copy(
            src_ref=ref, dst_ref=ref, send_sem=g_send.at[at], recv_sem=g_recv.at[at],
            device_id=device, device_id_type=MESH,
        )
        copy.start()
        sends.append(copy)

    def landed(part, chunk, slot, ref):
        pltpu.make_async_copy(ref, ref, g_recv.at[sem_at(part, chunk, slot)]).wait()

    mid = ROWS // 2

    def send_both(part, chunk, slot, ref, ring):
        send(part, chunk, slot, ref, ring[1])
        send(part, chunk, slot + 1, ref, ring[2])

    def pass_on(part, chunk, slot, below, above, ring, get):
        landed(part, chunk, slot, get(below, 0, ROWS))
        send(part, chunk, slot + 2, get(below, 0, mid), ring[1])
        landed(part, chunk, slot + 1, get(above, 0, ROWS))
        send(part, chunk, slot + 3, get(above, mid, ROWS - mid), ring[2])

    def second_direct(part, chunk, number, first_at):
        other = first_axis[1 - part]
        send_both(part, chunk, 4 + 4 * number, piece(part, chunk, first_at, other[0]), other)

    def second_forward(part, chunk, number, first_at):
        other = first_axis[1 - part]
        at = other[0]
        pass_on(
            part, chunk, 4 + 4 * number, (at + 3) % 4, (at + 1) % 4, other,
            lambda second_at, lo, size: piece(part, chunk, first_at, second_at, lo, size),
        )

    def step_own(chunk):
        for copy in x_copies[chunk]:
            copy.wait()
        for part in range(2):
            ring, other = first_axis[part], first_axis[1 - part]
            own = piece(part, chunk, ring[0], other[0])
            send_both(part, chunk, 0, own, ring)
        for part in range(2):
            second_direct(part, chunk, 0, first_axis[part][0])

    def step_near(chunk):
        for part in range(2):
            ring, other = first_axis[part], first_axis[1 - part]
            here = ring[0]
            pass_on(
                part, chunk, 0, (here + 3) % 4, (here + 1) % 4, ring,
                lambda first_at, lo, size: piece(part, chunk, first_at, other[0], lo, size),
            )
        for part in range(2):
            here = first_axis[part][0]
            second_direct(part, chunk, 1, (here + 3) % 4)
            second_direct(part, chunk, 2, (here + 1) % 4)
        for part in range(2):
            second_forward(part, chunk, 0, first_axis[part][0])

    def step_far(chunk):
        for part in range(2):
            ring, other = first_axis[part], first_axis[1 - part]
            far = (ring[0] + 2) % 4
            landed(part, chunk, 2, piece(part, chunk, far, other[0], 0, mid))
            landed(part, chunk, 3, piece(part, chunk, far, other[0], mid, ROWS - mid))
            second_direct(part, chunk, 3, far)
        for part in range(2):
            here = first_axis[part][0]
            second_forward(part, chunk, 1, (here + 3) % 4)
            second_forward(part, chunk, 2, (here + 1) % 4)

    def step_last(chunk):
        for part in range(2):
            second_forward(part, chunk, 3, (first_axis[part][0] + 2) % 4)

    def step_end(chunk):
        for part in range(2):
            here, far = first_axis[part][0], (first_axis[1 - part][0] + 2) % 4
            for number, first_at in enumerate((here, (here + 3) % 4, (here + 1) % 4, (here + 2) % 4)):
                landed(part, chunk, 6 + 4 * number, piece(part, chunk, first_at, far, 0, mid))
                landed(
                    part, chunk, 7 + 4 * number,
                    piece(part, chunk, first_at, far, mid, ROWS - mid),
                )

    start_x(0)
    start_x(1)
    for turn in range(CHUNKS + 4):
        for delay, step in enumerate((step_own, step_near, step_far, step_last, step_end)):
            if 0 <= turn - delay < CHUNKS:
                step(turn - delay)
                if delay == 0 and turn + 2 < CHUNKS:
                    start_x(turn + 2)

    for copy in sends:
        copy.wait_send()
    for copy in margin_sends:
        copy.wait_send()
    sent = slabs.at[pl.ds(0, 31)]
    pltpu.make_async_copy(sent, sent, t_send).wait()


def gathered(parent, margin, counts, factor, local_inverse):
    grid = parent.reshape(8, 4, 2, 64, BLOCK).transpose(0, 3, 1, 2, 4)
    dma = pltpu.SemaphoreType.DMA
    vmem = pl.BlockSpec(memory_space=pltpu.VMEM)
    hbm = pl.BlockSpec(memory_space=pltpu.HBM)
    return pl.pallas_call(
        gather_kernel,
        out_shape=(
            jax.ShapeDtypeStruct((2, NOV, 9, 4, 4, 4, 2, BLOCK), jnp.bfloat16),
            jax.ShapeDtypeStruct((2, 4096, 256), jnp.bfloat16),
            jax.ShapeDtypeStruct((2, 256, 4096), jnp.bfloat16),
            jax.ShapeDtypeStruct((2, 256, 256), jnp.float32),
        ),
        in_specs=[hbm] * 5,
        out_specs=(vmem,) * 4,
        scratch_shapes=[
            pltpu.VMEM(grid.shape, jnp.bfloat16),
            pltpu.VMEM(factor.shape, jnp.bfloat16),
            pltpu.VMEM(local_inverse.shape, jnp.bfloat16),
            pltpu.VMEM((64, 64, 2, BLOCK), jnp.bfloat16),
            pltpu.VMEM((4, 2, NOV, 9, 2, BLOCK), jnp.bfloat16),
            pltpu.VMEM((4, 2, NOV), jnp.int32),
            pltpu.SMEM((4, 2, NOV), jnp.int32),
            pltpu.SMEM((2,), jnp.int32),
            dma, dma((4,)), dma((4,)), dma((4,)), dma((4,)), dma((4,)), dma((5,)),
            dma((4 * CHUNKS,)), dma((4 * CHUNKS,)),
            dma((2 * SLOTS * CHUNKS,)), dma((2 * SLOTS * CHUNKS,)),
        ],
        compiler_params=pltpu.CompilerParams(
            collective_id=0, has_side_effects=True, vmem_limit_bytes=28 * 2**20
        ),
        cost_estimate=pl.CostEstimate(
            flops=2 * 10**9, bytes_accessed=20 * 2**20, transcendentals=0
        ),
    )(*[
        pltpu.with_memory_space_constraint(value, pltpu.HBM)
        for value in (counts, grid, margin, factor, local_inverse)
    ])


def update_kernel(counts_ref, sub_ref, live_ref, flipped_ref, local_ref, coupling_ref, diag_ref):
    part = pl.program_id(0)
    count = counts_ref[part]

    def pair(index, total, late):
        a = 2 * index
        rows = pl.multiple_of(a * BLOCK, 2 * BLOCK)
        zero = jnp.zeros((BLOCK, BLOCK), jnp.bfloat16)
        wide = 8 if late else 9
        deep = 8 if late else 7

        def block(r, d):
            return sub_ref[part, (r + NOV) % NOV, d]

        direct = jnp.concatenate(
            [
                jnp.concatenate([block(a, d) for d in range(wide)] + [zero], axis=1),
                jnp.concatenate([zero] + [block(a + 1, d) for d in range(wide)], axis=1),
            ],
            axis=0,
        )
        result = jnp.dot(
            direct, live_ref[part, pl.ds(rows, (wide + 1) * BLOCK), :],
            preferred_element_type=jnp.float32,
        )
        mirrored = jnp.concatenate(
            [
                jnp.concatenate([block(a - d, d), block(a - d, d + 1) if d < deep else zero], axis=1)
                if d
                else jnp.concatenate([zero, block(a, 1)], axis=1)
                for d in range(deep, -1, -1)
            ],
            axis=0,
        )
        start = pl.multiple_of(rows + (NOV - deep) * BLOCK, BLOCK)
        turned = jnp.dot(
            flipped_ref[part, :, pl.ds(start, (deep + 1) * BLOCK)], mirrored,
            preferred_element_type=jnp.float32,
        )
        result = -(result + turned.T)
        block_at = a + lax.broadcasted_iota(jnp.int32, result.shape, 0) // BLOCK
        result = jnp.where(block_at < count, result, jnp.zeros_like(result)).astype(jnp.bfloat16)
        coupling_ref[0, pl.ds(rows, 2 * BLOCK), :] = result
        return total - jnp.dot(
            flipped_ref[part, :, pl.ds(rows, 2 * BLOCK)], result,
            preferred_element_type=jnp.float32,
        )

    total = local_ref[part]
    total = lax.fori_loop(0, 4, functools.partial(pair, late=False), total, unroll=4)
    total = lax.fori_loop(4, 8, functools.partial(pair, late=True), total, unroll=4)
    for c in range(2):
        at = slice(c * BLOCK, (c + 1) * BLOCK)
        diag_ref[0, c] = total[at, at]


def body(parent, margin, counts, factor, local_inverse):
    sub, live, flipped, local = gathered(parent, margin, counts, factor, local_inverse)
    vmem = pl.BlockSpec(memory_space=pltpu.VMEM)
    return pl.pallas_call(
        update_kernel,
        grid=(2,),
        out_shape=(
            jax.ShapeDtypeStruct(factor.shape, jnp.bfloat16),
            jax.ShapeDtypeStruct((2, 2, BLOCK, BLOCK), jnp.float32),
        ),
        in_specs=[pl.BlockSpec(memory_space=pltpu.SMEM), vmem, vmem, vmem, vmem],
        out_specs=(
            pl.BlockSpec((1, 2048, 256), lambda f: (f, 0, 0)),
            pl.BlockSpec((1, 2, BLOCK, BLOCK), lambda f: (f, 0, 0, 0)),
        ),
        compiler_params=pltpu.CompilerParams(vmem_limit_bytes=16 * 2**20),
        cost_estimate=pl.CostEstimate(
            flops=6 * 10**9, bytes_accessed=20 * 2**20, transcendentals=0
        ),
    )(counts, sub.reshape(2, NOV, 9, BLOCK, BLOCK), live, flipped, local)


def solution(mesh):
    placed = (
        P(("front", "row"), None),
        P("front", None),
        P("front"),
        P("front", None, "row"),
        P("front", None, "row"),
    )
    return jax.shard_map(
        body,
        mesh=mesh,
        in_specs=placed,
        out_specs=(P("front", None, "row"), P("front", "row", None, None)),
        check_vma=False,
    )
```

```python
import functools

import jax
import jax.numpy as jnp
from jax import lax
from jax.experimental import pallas as pl
from jax.experimental.pallas import tpu as pltpu
from jax.sharding import PartitionSpec as P

MESH = pl.DeviceIdType.MESH
NOV = 16
BLOCK = 128
CHUNKS = 4
SLOTS = 20
ROWS = NOV // CHUNKS


def place(x, core, y, z):
    return (2 * x + core, 4 * z + y)


def band(chunk):
    return 9 if chunk < CHUNKS // 2 else 8


def partners(x, core, y, z, up):
    return place(x, core, (y + up * (1 - core)) % 4, (z + up * core) % 4)


def others(x, core, y, z, up):
    return place(x, core, (y + up * core) % 4, (z + up * (1 - core)) % 4)


def prepare_factor(count, part, factor_buf, lent_buf, live_ref, flipped_ref):
    def mask(a, _):
        rows = pl.multiple_of(a * BLOCK, BLOCK)
        value = jnp.concatenate(
            [
                factor_buf[part, pl.ds(rows, BLOCK), :],
                lent_buf[0, pl.ds(rows, BLOCK), :],
                lent_buf[1, pl.ds(rows, BLOCK), :],
            ],
            axis=1,
        )
        value = jnp.where(a < count, value, jnp.zeros_like(value))
        turned = value.T
        for lap in range(2):
            at = pl.multiple_of(rows + lap * NOV * BLOCK, BLOCK)
            live_ref[pl.ds(at, BLOCK), :] = value
            flipped_ref[:, pl.ds(at, BLOCK)] = turned
        return 0

    lax.fori_loop(0, NOV, mask, 0)


def prepare_local(part, first_col, inverse_buf, local_ref):
    def local(step, total):
        rows = pl.multiple_of(step * 512, 512)
        value = inverse_buf[part, pl.ds(rows, 512), :]
        row_at = rows + lax.broadcasted_iota(jnp.int32, value.shape, 0)
        col_at = first_col + lax.broadcasted_iota(jnp.int32, value.shape, 1)
        value = jnp.where(row_at >= col_at, value, jnp.zeros_like(value))
        return total + lax.dot_general(
            value, value, (((0,), (0,)), ((), ())), preferred_element_type=jnp.float32
        )

    local_ref[part] = lax.fori_loop(0, 8, local, jnp.zeros((256, 256), jnp.float32))


def gather_kernel(
    counts_ref, parent_ref, margin_ref, factor_ref, inverse_ref,
    out_ref, live_ref, flipped_ref, local_ref,
    parent_buf, factor_buf, inverse_buf, lent_buf, other_buf, slabs, picked, margin_buf, margin_smem, counts_smem,
    t_send, t_recv, d_send, d_recv, m_send, m_recv, l_sem, f_send, f_recv, x_send, x_recv, g_send, g_recv,
):
    front = lax.axis_index("front")
    row = lax.axis_index("row")
    x, core = front // 2, front % 2
    z, y = row // 4, row % 4
    half, yh = y % 2, y // 2
    fold = half * 2 + yh
    me_q = yh * 16 + z * 4 + x
    my_block = 16 * x + 8 * core + 2 * z + yh
    here = y * (1 - core) + z * core
    there = z * (1 - core) + y * core
    mine = here % 2
    sibling = place(x, 1 - core, y, z)
    pair_up = partners(x, core, y, z, 1)
    pair_down = partners(x, core, y, z, 3)
    pair_far = partners(x, core, y, z, 2)
    ring_up = others(x, core, y, z, 1)
    ring_down = others(x, core, y, z, 3)
    y_up = place(x, core, (y + 1) % 4, z)
    y_down = place(x, core, (y + 3) % 4, z)

    def member(q):
        return place(q % 4, core, 2 * (q // 16) + half, (q // 4) % 4)

    parent_load = pltpu.make_async_copy(parent_ref, parent_buf, l_sem.at[0])
    parent_load.start()
    factor_load = pltpu.make_async_copy(factor_ref, factor_buf, l_sem.at[1])
    factor_load.start()
    inverse_load = pltpu.make_async_copy(inverse_ref, inverse_buf, l_sem.at[2])
    inverse_load.start()
    counts_load = pltpu.make_async_copy(counts_ref, counts_smem, l_sem.at[4])
    counts_load.start()

    barrier = pltpu.get_barrier_semaphore()

    def greet(step, _):
        pl.semaphore_signal(
            barrier, inc=1, device_id=member((me_q + step) % 32), device_id_type=MESH
        )
        return 0

    lax.fori_loop(1, 32, greet, 0)
    for other in (sibling, y_up, y_down):
        pl.semaphore_signal(barrier, inc=1, device_id=other, device_id_type=MESH)
    parent_load.wait()
    pl.semaphore_wait(barrier, 34)

    margin_sends = []
    for step in (1, 2, 3):
        copy = pltpu.make_async_remote_copy(
            src_ref=margin_ref,
            dst_ref=margin_buf.at[x],
            send_sem=m_send.at[step],
            recv_sem=m_recv.at[x],
            device_id=place((x + step) % 4, core, y, z),
            device_id_type=MESH,
        )
        copy.start()
        margin_sends.append(copy)
    pltpu.make_async_copy(margin_ref, margin_buf.at[x], m_recv.at[x]).start()
    pltpu.make_async_copy(
        parent_buf.at[me_q // 4, :, me_q % 4], slabs.at[my_block], t_recv.at[x]
    ).start()

    for offset in (0, 1, 3, 2):

        def spread(step, _):
            q = (yh * 4 + z + step) % 8 * 4 + (x + offset) % 4
            pltpu.make_async_remote_copy(
                src_ref=parent_buf.at[q // 4, :, q % 4],
                dst_ref=slabs.at[my_block],
                send_sem=t_send,
                recv_sem=t_recv.at[x],
                device_id=member(q),
                device_id_type=MESH,
            ).start()
            return 0

        lax.fori_loop(0 if offset else 1, 8, spread, 0)

    for source in range(4):
        pltpu.make_async_copy(margin_ref, margin_buf.at[source], m_recv.at[source]).wait()
    to_smem = pltpu.make_async_copy(margin_buf, margin_smem, l_sem.at[3])
    to_smem.start()
    to_smem.wait()

    exchanges = []
    for offset in (0, 1, 3, 2):
        source = (x + 4 - offset) % 4
        group = slabs.at[pl.ds(16 * source + 8 * core, 8)]
        pltpu.make_async_copy(group, group, t_recv.at[source]).wait()
        copy = pltpu.make_async_remote_copy(
            src_ref=group,
            dst_ref=group,
            send_sem=d_send.at[source],
            recv_sem=d_recv.at[source],
            device_id=sibling,
            device_id_type=MESH,
        )
        copy.start()
        exchanges.append(copy)

    factor_load.wait()
    lends = []
    for number, device in enumerate((pair_up, pair_down)):
        copy = pltpu.make_async_remote_copy(
            src_ref=factor_buf.at[1 - mine, :, pl.ds(number * BLOCK, BLOCK)],
            dst_ref=lent_buf.at[number],
            send_sem=f_send.at[number],
            recv_sem=f_recv.at[number],
            device_id=device,
            device_id_type=MESH,
        )
        copy.start()
        lends.append(copy)

    for copy in exchanges:
        copy.wait()

    def span(chunk):
        return pl.ds(chunk * ROWS, ROWS), pl.ds(0, band(chunk))

    x_copies = [[] for _ in range(CHUNKS)]

    def start_x(chunk):
        rows, dists = span(chunk)
        for step in (2, 1, 3, 0):
            target = (x + step) % 4

            def pick(index, _):
                part, a = index // ROWS, chunk * ROWS + index % ROWS
                block_row = margin_smem[target, part, a]
                for d in range(band(chunk)):
                    block_col = margin_smem[target, part, (a + d) % NOV]
                    picked[target, part, a, d] = slabs[block_row, block_col]
                return 0

            lax.fori_loop(0, 2 * ROWS, pick, 0)
            slot = 8 * chunk + 2 * step
            lands = (out_ref.at[rows, dists, fold, z, x], other_buf.at[rows, dists, x])
            for number, land in enumerate(lands):
                part = (mine + number) % 2
                if step:
                    copy = pltpu.make_async_remote_copy(
                        src_ref=picked.at[target, part, rows, dists],
                        dst_ref=land,
                        send_sem=x_send.at[slot + number],
                        recv_sem=x_recv.at[slot + number],
                        device_id=place(target, core, y, z),
                        device_id_type=MESH,
                    )
                else:
                    copy = pltpu.make_async_copy(
                        picked.at[target, part, rows, dists], land, x_recv.at[slot + number]
                    )
                copy.start()
                x_copies[chunk].append(copy)

    sends = []

    def piece(chunk, pair_at, ring_at, lo=0, size=ROWS):
        y_at = pair_at * (1 - core) + ring_at * core
        z_at = ring_at * (1 - core) + pair_at * core
        return out_ref.at[
            pl.ds(chunk * ROWS + lo, size), pl.ds(0, band(chunk)),
            (y_at % 2) * 2 + y_at // 2, z_at,
        ]

    def send(chunk, slot, source, target, device):
        at = SLOTS * chunk + slot
        copy = pltpu.make_async_remote_copy(
            src_ref=source, dst_ref=target, send_sem=g_send.at[at], recv_sem=g_recv.at[at],
            device_id=device, device_id_type=MESH,
        )
        copy.start()
        sends.append(copy)

    def landed(chunk, slot, ref):
        pltpu.make_async_copy(ref, ref, g_recv.at[SLOTS * chunk + slot]).wait()

    mid = ROWS // 2
    pair_places = (here, (here + 3) % 4, (here + 1) % 4, (here + 2) % 4)
    above, below, far = (there + 1) % 4, (there + 3) % 4, (there + 2) % 4

    def ring_direct(chunk, number):
        own = piece(chunk, pair_places[number], there)
        send(chunk, 4 + 4 * number, own, own, ring_up)
        send(chunk, 5 + 4 * number, own, own, ring_down)

    def ring_forward(chunk, number):
        at = pair_places[number]
        landed(chunk, 4 + 4 * number, piece(chunk, at, below))
        low = piece(chunk, at, below, 0, mid)
        send(chunk, 6 + 4 * number, low, low, ring_up)
        landed(chunk, 5 + 4 * number, piece(chunk, at, above))
        high = piece(chunk, at, above, mid, ROWS - mid)
        send(chunk, 7 + 4 * number, high, high, ring_down)

    def step_own(chunk):
        rows, dists = span(chunk)
        for copy in x_copies[chunk]:
            copy.wait()
        own = piece(chunk, here, there)
        other = other_buf.at[rows, dists]
        send(chunk, 0, other, own, pair_up)
        send(chunk, 1, other, own, pair_down)
        send(chunk, 2, own, own, pair_far)
        ring_direct(chunk, 0)

    def step_near(chunk):
        for number in (1, 2, 3):
            landed(chunk, number - 1, piece(chunk, pair_places[number], there))
            ring_direct(chunk, number)
        ring_forward(chunk, 0)

    def step_far(chunk):
        for number in (1, 2, 3):
            ring_forward(chunk, number)

    def step_end(chunk):
        for number, at in enumerate(pair_places):
            landed(chunk, 6 + 4 * number, piece(chunk, at, far, 0, mid))
            landed(chunk, 7 + 4 * number, piece(chunk, at, far, mid, ROWS - mid))

    start_x(0)
    start_x(1)
    for turn in range(CHUNKS + 3):
        for delay, step in enumerate((step_own, step_near, step_far, step_end)):
            if 0 <= turn - delay < CHUNKS:
                step(turn - delay)
                if delay == 0 and turn + 2 < CHUNKS:
                    start_x(turn + 2)
        if turn == 1:
            for copy in lends:
                copy.wait()
            counts_load.wait()
            prepare_factor(counts_smem[mine], mine, factor_buf, lent_buf, live_ref, flipped_ref)
        if turn == 2:
            inverse_load.wait()
            for part in range(2):
                prepare_local(part, row * 256, inverse_buf, local_ref)

    for copy in sends:
        copy.wait_send()
    for copy in margin_sends:
        copy.wait_send()
    sent = slabs.at[pl.ds(0, 31)]
    pltpu.make_async_copy(sent, sent, t_send).wait()


def gathered(parent, margin, counts, factor, local_inverse):
    grid = parent.reshape(8, 4, 2, 64, BLOCK).transpose(0, 3, 1, 2, 4)
    dma = pltpu.SemaphoreType.DMA
    vmem = pl.BlockSpec(memory_space=pltpu.VMEM)
    hbm = pl.BlockSpec(memory_space=pltpu.HBM)
    return pl.pallas_call(
        gather_kernel,
        out_shape=(
            jax.ShapeDtypeStruct((NOV, 9, 4, 4, 4, 2, BLOCK), jnp.bfloat16),
            jax.ShapeDtypeStruct((4096, 512), jnp.bfloat16),
            jax.ShapeDtypeStruct((512, 4096), jnp.bfloat16),
            jax.ShapeDtypeStruct((2, 256, 256), jnp.float32),
        ),
        in_specs=[hbm] * 5,
        out_specs=(vmem,) * 4,
        scratch_shapes=[
            pltpu.VMEM(grid.shape, jnp.bfloat16),
            pltpu.VMEM(factor.shape, jnp.bfloat16),
            pltpu.VMEM(local_inverse.shape, jnp.bfloat16),
            pltpu.VMEM((2, 2048, BLOCK), jnp.bfloat16),
            pltpu.VMEM((NOV, 9, 4, 2, BLOCK), jnp.bfloat16),
            pltpu.VMEM((64, 64, 2, BLOCK), jnp.bfloat16),
            pltpu.VMEM((4, 2, NOV, 9, 2, BLOCK), jnp.bfloat16),
            pltpu.VMEM((4, 2, NOV), jnp.int32),
            pltpu.SMEM((4, 2, NOV), jnp.int32),
            pltpu.SMEM((2,), jnp.int32),
            dma, dma((4,)), dma((4,)), dma((4,)), dma((4,)), dma((4,)), dma((5,)),
            dma((2,)), dma((2,)), dma((8 * CHUNKS,)), dma((8 * CHUNKS,)),
            dma((SLOTS * CHUNKS,)), dma((SLOTS * CHUNKS,)),
        ],
        compiler_params=pltpu.CompilerParams(
            collective_id=0, has_side_effects=True, vmem_limit_bytes=28 * 2**20
        ),
        cost_estimate=pl.CostEstimate(
            flops=2 * 10**9, bytes_accessed=20 * 2**20, transcendentals=0
        ),
    )(*[
        pltpu.with_memory_space_constraint(value, pltpu.HBM)
        for value in (counts, grid, margin, factor, local_inverse)
    ])


def update_kernel(
    counts_ref, sub_ref, live_ref, flipped_ref, local_ref, coupling_ref, diag_ref,
    stage, cross_out, cross_in, c_send, c_recv, k_send, k_recv,
):
    front = lax.axis_index("front")
    row = lax.axis_index("row")
    x, core = front // 2, front % 2
    z, y = row // 4, row % 4
    mine = (y * (1 - core) + z * core) % 2
    count = counts_ref[mine]
    pair_up = partners(x, core, y, z, 1)
    pair_down = partners(x, core, y, z, 3)
    barrier = pltpu.get_barrier_semaphore()
    for other in (pair_up, pair_down):
        pl.semaphore_signal(barrier, inc=1, device_id=other, device_id_type=MESH)

    zero = jnp.zeros((BLOCK, BLOCK), jnp.bfloat16)
    totals = [jnp.zeros((256, 256), jnp.float32) for _ in range(2)]
    sends = []

    def pair(index):
        a = 2 * index
        wide = 8 if index >= 4 else 9
        deep = 8 if index >= 4 else 7

        def block(r, d):
            return sub_ref[r % NOV, d]

        direct = jnp.concatenate(
            [
                jnp.concatenate([block(a, d) for d in range(wide)] + [zero], axis=1),
                jnp.concatenate([zero] + [block(a + 1, d) for d in range(wide)], axis=1),
            ],
            axis=0,
        )
        result = jnp.dot(
            direct, live_ref[a * BLOCK : (a + wide + 1) * BLOCK, :],
            preferred_element_type=jnp.float32,
        )
        mirrored = jnp.concatenate(
            [
                jnp.concatenate([block(a - d, d), block(a - d, d + 1) if d < deep else zero], axis=1)
                if d
                else jnp.concatenate([zero, block(a, 1)], axis=1)
                for d in range(deep, -1, -1)
            ],
            axis=0,
        )
        start = (a + NOV - deep) * BLOCK
        turned = jnp.dot(
            flipped_ref[:, start : start + (deep + 1) * BLOCK], mirrored,
            preferred_element_type=jnp.float32,
        )
        result = -(result + turned.T)
        block_at = a + lax.broadcasted_iota(jnp.int32, result.shape, 0) // BLOCK
        return jnp.where(block_at < count, result, jnp.zeros_like(result)).astype(jnp.bfloat16)

    def send(source, target, send_sem, recv_sem, device):
        copy = pltpu.make_async_remote_copy(
            src_ref=source, dst_ref=target, send_sem=send_sem, recv_sem=recv_sem,
            device_id=device, device_id_type=MESH,
        )
        copy.start()
        sends.append(copy)

    def returned(part, first, number):
        return coupling_ref.at[
            part, pl.ds(first, 512), pl.ds(number * BLOCK, BLOCK)
        ]

    for index in range(8):
        rows = slice(2 * index * BLOCK, (2 * index + 2) * BLOCK)
        result = pair(index)
        coupling_ref[mine, rows, :] = result[:, :256]
        stage[0, rows, :] = result[:, 256:384]
        stage[1, rows, :] = result[:, 384:]
        for number in range(2):
            at = slice(256 * number, 256 * number + 256)
            totals[number] -= jnp.dot(
                flipped_ref[at, rows], result[:, at], preferred_element_type=jnp.float32
            )
        if index == 1:
            pl.semaphore_wait(barrier, 2)
        if index % 2:
            first = (index - 1) * 2 * BLOCK
            for number, device in enumerate((pair_down, pair_up)):
                slot = 2 * (index // 2) + number
                send(
                    stage.at[number, pl.ds(first, 512)], returned(mine, first, number),
                    c_send.at[slot], c_recv.at[slot], device,
                )

    for number, device in enumerate((pair_down, pair_up)):
        at = slice(number * BLOCK, (number + 1) * BLOCK)
        cross_out[number] = totals[1][at, at]
        send(
            cross_out.at[number], cross_in.at[number],
            k_send.at[number], k_recv.at[number], device,
        )
    for number in range(2):
        at = slice(number * BLOCK, (number + 1) * BLOCK)
        diag_ref[mine, number] = local_ref[mine, at, at] + totals[0][at, at]
    for number in range(2):
        at = slice(number * BLOCK, (number + 1) * BLOCK)
        pltpu.make_async_copy(cross_in.at[number], cross_in.at[number], k_recv.at[number]).wait()
        diag_ref[1 - mine, number] = local_ref[1 - mine, at, at] + cross_in[number]
    for quarter in range(4):
        for number in range(2):
            ref = returned(1 - mine, quarter * 512, number)
            pltpu.make_async_copy(ref, ref, c_recv.at[2 * quarter + number]).wait()
    for copy in sends:
        copy.wait_send()


def body(parent, margin, counts, factor, local_inverse):
    sub, live, flipped, local = gathered(parent, margin, counts, factor, local_inverse)
    vmem = pl.BlockSpec(memory_space=pltpu.VMEM)
    dma = pltpu.SemaphoreType.DMA
    return pl.pallas_call(
        update_kernel,
        out_shape=(
            jax.ShapeDtypeStruct(factor.shape, jnp.bfloat16),
            jax.ShapeDtypeStruct((2, 2, BLOCK, BLOCK), jnp.float32),
        ),
        in_specs=[pl.BlockSpec(memory_space=pltpu.SMEM), vmem, vmem, vmem, vmem],
        out_specs=(vmem, vmem),
        scratch_shapes=[
            pltpu.VMEM((2, 2048, BLOCK), jnp.bfloat16),
            pltpu.VMEM((2, BLOCK, BLOCK), jnp.float32),
            pltpu.VMEM((2, BLOCK, BLOCK), jnp.float32),
            dma((8,)), dma((8,)), dma((2,)), dma((2,)),
        ],
        compiler_params=pltpu.CompilerParams(
            collective_id=1, has_side_effects=True, vmem_limit_bytes=24 * 2**20
        ),
        cost_estimate=pl.CostEstimate(
            flops=6 * 10**9, bytes_accessed=20 * 2**20, transcendentals=0
        ),
    )(counts, sub.reshape(NOV, 9, BLOCK, BLOCK), live, flipped, local)


def solution(mesh):
    placed = (
        P(("front", "row"), None),
        P("front", None),
        P("front"),
        P("front", None, "row"),
        P("front", None, "row"),
    )
    return jax.shard_map(
        body,
        mesh=mesh,
        in_specs=placed,
        out_specs=(P("front", None, "row"), P("front", "row", None, None)),
        check_vma=False,
    )
```

```python
import functools

import jax
import jax.numpy as jnp
from jax import lax
from jax.experimental import pallas as pl
from jax.experimental.pallas import tpu as pltpu
from jax.sharding import PartitionSpec as P

MESH = pl.DeviceIdType.MESH
NOV = 16
BLOCK = 128
BLOCKS = 136
CUTS = (0, 5, 16)
CHUNKS = len(CUTS) - 1
SLOTS = 20


def place(x, core, y, z):
    return (2 * x + core, 4 * z + y)


def first_block(a):
    return NOV * a - a * (a - 1) // 2


def order(block):
    x, core, z, yh = block >> 4, (block >> 3) & 1, (block >> 1) & 3, block & 1
    group = z * (1 - core) + (7 - z) * core
    return group * 8 + x * 2 + yh


def network(count):
    swaps, p = [], 1
    while p < count:
        k = p
        while k >= 1:
            for j in range(k % p, count - k, 2 * k):
                for i in range(min(k, count - j - k)):
                    if (i + j) // (2 * p) == (i + j + k) // (2 * p):
                        swaps.append((i + j, i + j + k))
            k //= 2
        p *= 2
    return swaps


def columns(core, z):
    return (2 * z, 16 - 2 * z) if core == 0 else (8, 2 * z + 2)


def spans(chunk):
    first, last = first_block(CUTS[chunk]), first_block(CUTS[chunk + 1])
    return first, last - first


def partners(x, core, y, z, up):
    return place(x, core, (y + up * (1 - core)) % 4, (z + up * core) % 4)


def others(x, core, y, z, up):
    return place(x, core, (y + up * core) % 4, (z + up * (1 - core)) % 4)


def prepare_factor(
    count, part, ranked, factor_buf, lent_buf, live_ref, flipped_ref, alive_ref
):
    def mask(at, _):
        a = ranked(at)
        rows = pl.multiple_of(at * BLOCK, BLOCK)
        value = jnp.concatenate([factor_buf[part, a], lent_buf[0, a], lent_buf[1, a]], axis=1)
        value = jnp.where(a < count, value, jnp.zeros_like(value))
        live_ref[pl.ds(rows, BLOCK), :] = value
        flipped_ref[:, pl.ds(rows, BLOCK)] = value.T
        ones = jnp.ones((8, 512), jnp.float32)
        alive_ref[at] = jnp.where(a < count, ones, jnp.zeros_like(ones))
        return 0

    lax.fori_loop(0, NOV, mask, 0)


def prepare_local(part, first_col, inverse_buf, local_ref):
    def local(step, total):
        rows = pl.multiple_of(step * 512, 512)
        value = inverse_buf[part, pl.ds(rows, 512), :]
        row_at = rows + lax.broadcasted_iota(jnp.int32, value.shape, 0)
        col_at = first_col + lax.broadcasted_iota(jnp.int32, value.shape, 1)
        value = jnp.where(row_at >= col_at, value, jnp.zeros_like(value))
        return total + lax.dot_general(
            value, value, (((0,), (0,)), ((), ())), preferred_element_type=jnp.float32
        )

    local_ref[part] = lax.fori_loop(0, 8, local, jnp.zeros((256, 256), jnp.float32))


def gather_kernel(
    counts_ref, parent_ref, margin_ref, factor_ref, inverse_ref,
    out_ref, live_ref, flipped_ref, alive_ref, local_ref,
    parent_buf, factor_buf, inverse_buf, lent_buf, other_buf, slabs, picked, margin_buf, margin_smem, sorted_smem, ranked_smem, counts_smem,
    t_send, t_recv, d_send, d_recv, m_send, m_recv, l_sem, f_send, f_recv, x_send, x_recv, g_send, g_recv,
):
    front = lax.axis_index("front")
    row = lax.axis_index("row")
    x, core = front // 2, front % 2
    z, y = row // 4, row % 4
    half, yh = y % 2, y // 2
    fold = half * 2 + yh
    me_q = yh * 16 + z * 4 + x
    my_block = 16 * x + 8 * core + 2 * z + yh
    here = y * (1 - core) + z * core
    there = z * (1 - core) + y * core
    mine = here % 2
    sibling = place(x, 1 - core, y, z)
    pair_up = partners(x, core, y, z, 1)
    pair_down = partners(x, core, y, z, 3)
    pair_far = partners(x, core, y, z, 2)
    ring_up = others(x, core, y, z, 1)
    ring_down = others(x, core, y, z, 3)
    y_up = place(x, core, (y + 1) % 4, z)
    y_down = place(x, core, (y + 3) % 4, z)

    def member(q):
        return place(q % 4, core, 2 * (q // 16) + half, (q // 4) % 4)

    parent_load = pltpu.make_async_copy(parent_ref, parent_buf, l_sem.at[0])
    parent_load.start()
    factor_load = pltpu.make_async_copy(factor_ref, factor_buf, l_sem.at[1])
    factor_load.start()
    inverse_load = pltpu.make_async_copy(inverse_ref, inverse_buf, l_sem.at[2])
    inverse_load.start()
    counts_load = pltpu.make_async_copy(counts_ref, counts_smem, l_sem.at[4])
    counts_load.start()

    barrier = pltpu.get_barrier_semaphore()

    def greet(step, _):
        pl.semaphore_signal(
            barrier, inc=1, device_id=member((me_q + step) % 32), device_id_type=MESH
        )
        return 0

    lax.fori_loop(1, 32, greet, 0)
    for other in (sibling, y_up, y_down):
        pl.semaphore_signal(barrier, inc=1, device_id=other, device_id_type=MESH)
    parent_load.wait()
    pl.semaphore_wait(barrier, 34)

    margin_sends = []
    for step in (1, 2, 3):
        copy = pltpu.make_async_remote_copy(
            src_ref=margin_ref,
            dst_ref=margin_buf.at[x],
            send_sem=m_send.at[step],
            recv_sem=m_recv.at[x],
            device_id=place((x + step) % 4, core, y, z),
            device_id_type=MESH,
        )
        copy.start()
        margin_sends.append(copy)
    pltpu.make_async_copy(margin_ref, margin_buf.at[x], m_recv.at[x]).start()

    def spread_all(own_core, own_z):
        cols = pl.ds(*columns(own_core, own_z))
        pltpu.make_async_copy(
            parent_buf.at[me_q // 4, :, cols, me_q % 4],
            slabs.at[my_block, :, cols],
            t_recv.at[x],
        ).start()
        for offset in (0, 1, 3, 2):

            def spread(step, _):
                q = (yh * 4 + z + step) % 8 * 4 + (x + offset) % 4
                pltpu.make_async_remote_copy(
                    src_ref=parent_buf.at[q // 4, :, cols, q % 4],
                    dst_ref=slabs.at[my_block, :, cols],
                    send_sem=t_send,
                    recv_sem=t_recv.at[x],
                    device_id=member(q),
                    device_id_type=MESH,
                ).start()
                return 0

            lax.fori_loop(0 if offset else 1, 8, spread, 0)

    for own_core in range(2):
        for own_z in range(4):
            pl.when(jnp.logical_and(core == own_core, z == own_z))(
                functools.partial(spread_all, own_core, own_z)
            )

    for source in range(4):
        pltpu.make_async_copy(margin_ref, margin_buf.at[source], m_recv.at[source]).wait()
    to_smem = pltpu.make_async_copy(margin_buf, margin_smem, l_sem.at[3])
    to_smem.start()
    to_smem.wait()

    swaps = network(NOV)

    def sort(index, _):
        target, part = index // 2, index % 2
        keys = []
        for a in range(NOV):
            block = margin_smem[target, part, a]
            keys.append(order(block) * 1024 + block * NOV + a)
        for i, j in swaps:
            keys[i], keys[j] = jnp.minimum(keys[i], keys[j]), jnp.maximum(keys[i], keys[j])
        for a in range(NOV):
            sorted_smem[target, part, a] = (keys[a] >> 4) & 63
            ranked_smem[target, part, a] = keys[a] & (NOV - 1)
        return 0

    lax.fori_loop(0, 8, sort, 0)

    def swap_cores(own_core, wait_only):
        total = sum(columns(own_core, own_z)[1] for own_z in range(4)) // 4
        for offset in (0, 1, 3, 2):
            source = (x + 4 - offset) % 4
            if not wait_only:
                group = slabs.at[pl.ds(0, 8), :, pl.ds(0, total)]
                pltpu.make_async_copy(group, group, t_recv.at[source]).wait()
            for own_z in range(4):
                part = slabs.at[
                    pl.ds(16 * source + 8 * own_core + 2 * own_z, 2), :,
                    pl.ds(*columns(own_core, own_z)),
                ]
                slot = 4 * source + own_z
                if wait_only:
                    pltpu.make_async_copy(part, part, d_recv.at[slot]).wait()
                else:
                    pltpu.make_async_remote_copy(
                        src_ref=part,
                        dst_ref=part,
                        send_sem=d_send.at[slot],
                        recv_sem=d_recv.at[slot],
                        device_id=sibling,
                        device_id_type=MESH,
                    ).start()

    def swap_sent(own_core):
        for source in range(4):
            for own_z in range(4):
                part = slabs.at[
                    pl.ds(16 * source + 8 * own_core + 2 * own_z, 2), :,
                    pl.ds(*columns(own_core, own_z)),
                ]
                pltpu.make_async_copy(part, part, d_send.at[4 * source + own_z]).wait()

    for own_core in range(2):
        pl.when(core == own_core)(functools.partial(swap_cores, own_core, False))

    factor_load.wait()
    lends = []
    for number, device in enumerate((pair_up, pair_down)):
        copy = pltpu.make_async_remote_copy(
            src_ref=factor_buf.at[1 - mine, :, :, pl.ds(number * BLOCK, BLOCK)],
            dst_ref=lent_buf.at[number],
            send_sem=f_send.at[number],
            recv_sem=f_recv.at[number],
            device_id=device,
            device_id_type=MESH,
        )
        copy.start()
        lends.append(copy)

    for own_core in range(2):
        pl.when(core == 1 - own_core)(functools.partial(swap_cores, own_core, True))

    x_copies = [[] for _ in range(CHUNKS)]

    def start_x(chunk):
        blocks = pl.ds(*spans(chunk))
        for step in (2, 1, 3, 0):
            target = (x + step) % 4

            def pick(part, _):
                ids = [sorted_smem[target, part, a] for a in range(NOV)]
                for a in range(CUTS[chunk], CUTS[chunk + 1]):
                    for b in range(a, NOV):
                        block = slabs[ids[a], ids[b] >> 4, ids[b] & 15]
                        picked[target, part, first_block(a) + b - a] = block
                return 0

            lax.fori_loop(0, 2, pick, 0)
            slot = 8 * chunk + 2 * step
            lands = (out_ref.at[blocks, fold, z, x], other_buf.at[blocks, x])
            for number, land in enumerate(lands):
                part = (mine + number) % 2
                if step:
                    copy = pltpu.make_async_remote_copy(
                        src_ref=picked.at[target, part, blocks],
                        dst_ref=land,
                        send_sem=x_send.at[slot + number],
                        recv_sem=x_recv.at[slot + number],
                        device_id=place(target, core, y, z),
                        device_id_type=MESH,
                    )
                else:
                    copy = pltpu.make_async_copy(
                        picked.at[target, part, blocks], land, x_recv.at[slot + number]
                    )
                copy.start()
                x_copies[chunk].append(copy)

    sends = []

    def piece(chunk, pair_at, ring_at, side=None):
        y_at = pair_at * (1 - core) + ring_at * core
        z_at = ring_at * (1 - core) + pair_at * core
        first, count = spans(chunk)
        if side == 0:
            count = count // 2
        if side == 1:
            first, count = first + count // 2, count - count // 2
        return out_ref.at[pl.ds(first, count), (y_at % 2) * 2 + y_at // 2, z_at]

    def send(chunk, slot, source, target, device):
        at = SLOTS * chunk + slot
        copy = pltpu.make_async_remote_copy(
            src_ref=source, dst_ref=target, send_sem=g_send.at[at], recv_sem=g_recv.at[at],
            device_id=device, device_id_type=MESH,
        )
        copy.start()
        sends.append(copy)

    def landed(chunk, slot, ref):
        pltpu.make_async_copy(ref, ref, g_recv.at[SLOTS * chunk + slot]).wait()

    pair_places = (here, (here + 3) % 4, (here + 1) % 4, (here + 2) % 4)
    above, below, far = (there + 1) % 4, (there + 3) % 4, (there + 2) % 4

    def ring_direct(chunk, number):
        own = piece(chunk, pair_places[number], there)
        send(chunk, 4 + 4 * number, own, own, ring_up)
        send(chunk, 5 + 4 * number, own, own, ring_down)

    def ring_forward(chunk, number):
        at = pair_places[number]
        landed(chunk, 4 + 4 * number, piece(chunk, at, below))
        low = piece(chunk, at, below, 0)
        send(chunk, 6 + 4 * number, low, low, ring_up)
        landed(chunk, 5 + 4 * number, piece(chunk, at, above))
        high = piece(chunk, at, above, 1)
        send(chunk, 7 + 4 * number, high, high, ring_down)

    def step_own(chunk):
        for copy in x_copies[chunk]:
            copy.wait()
        own = piece(chunk, here, there)
        other = other_buf.at[pl.ds(*spans(chunk))]
        send(chunk, 0, other, own, pair_up)
        send(chunk, 1, other, own, pair_down)
        send(chunk, 2, own, own, pair_far)
        ring_direct(chunk, 0)

    def step_near(chunk):
        for number in (1, 2, 3):
            landed(chunk, number - 1, piece(chunk, pair_places[number], there))
            ring_direct(chunk, number)
        ring_forward(chunk, 0)

    def step_far(chunk):
        for number in (1, 2, 3):
            ring_forward(chunk, number)

    def step_end(chunk):
        for number, at in enumerate(pair_places):
            landed(chunk, 6 + 4 * number, piece(chunk, at, far, 0))
            landed(chunk, 7 + 4 * number, piece(chunk, at, far, 1))

    start_x(0)
    start_x(1)
    for turn in range(CHUNKS + 3):
        for delay, step in enumerate((step_own, step_near, step_far, step_end)):
            if 0 <= turn - delay < CHUNKS:
                step(turn - delay)
                if delay == 0 and turn + 2 < CHUNKS:
                    start_x(turn + 2)
        if turn == min(1, CHUNKS - 1):
            for copy in lends:
                copy.wait()
            counts_load.wait()
            prepare_factor(
                counts_smem[mine], mine, lambda at: ranked_smem[x, mine, at],
                factor_buf, lent_buf, live_ref, flipped_ref, alive_ref,
            )
        if turn == min(2, CHUNKS):
            inverse_load.wait()
            for part in range(2):
                prepare_local(part, row * 256, inverse_buf, local_ref)

    for copy in sends:
        copy.wait_send()
    for copy in margin_sends:
        copy.wait_send()

    def spread_sent(own_core, own_z):
        sent = slabs.at[pl.ds(0, 31), :, pl.ds(0, columns(own_core, own_z)[1])]
        pltpu.make_async_copy(sent, sent, t_send).wait()

    for own_core in range(2):
        pl.when(core == own_core)(functools.partial(swap_sent, own_core))
        for own_z in range(4):
            pl.when(jnp.logical_and(core == own_core, z == own_z))(
                functools.partial(spread_sent, own_core, own_z)
            )


def gathered(parent, margin, counts, factor, local_inverse):
    grid = parent.reshape(8, 4, 2, 4, 16, BLOCK).transpose(0, 3, 4, 1, 2, 5)
    factor = factor.reshape(2, NOV, BLOCK, 256)
    dma = pltpu.SemaphoreType.DMA
    vmem = pl.BlockSpec(memory_space=pltpu.VMEM)
    hbm = pl.BlockSpec(memory_space=pltpu.HBM)
    return pl.pallas_call(
        gather_kernel,
        out_shape=(
            jax.ShapeDtypeStruct((BLOCKS, 4, 4, 4, 2, BLOCK), jnp.bfloat16),
            jax.ShapeDtypeStruct((2048, 512), jnp.bfloat16),
            jax.ShapeDtypeStruct((512, 2048), jnp.bfloat16),
            jax.ShapeDtypeStruct((NOV, 8, 512), jnp.float32),
            jax.ShapeDtypeStruct((2, 256, 256), jnp.float32),
        ),
        in_specs=[hbm] * 5,
        out_specs=(vmem,) * 5,
        scratch_shapes=[
            pltpu.VMEM(grid.shape, jnp.bfloat16),
            pltpu.VMEM(factor.shape, jnp.bfloat16),
            pltpu.VMEM(local_inverse.shape, jnp.bfloat16),
            pltpu.VMEM((2, NOV, BLOCK, BLOCK), jnp.bfloat16),
            pltpu.VMEM((BLOCKS, 4, 2, BLOCK), jnp.bfloat16),
            pltpu.VMEM((64, 4, 16, 2, BLOCK), jnp.bfloat16),
            pltpu.VMEM((4, 2, BLOCKS, 2, BLOCK), jnp.bfloat16),
            pltpu.VMEM((4, 2, NOV), jnp.int32),
            pltpu.SMEM((4, 2, NOV), jnp.int32),
            pltpu.SMEM((4, 2, NOV), jnp.int32),
            pltpu.SMEM((4, 2, NOV), jnp.int32),
            pltpu.SMEM((2,), jnp.int32),
            dma, dma((4,)), dma((16,)), dma((16,)), dma((4,)), dma((4,)), dma((5,)),
            dma((2,)), dma((2,)), dma((8 * CHUNKS,)), dma((8 * CHUNKS,)),
            dma((SLOTS * CHUNKS,)), dma((SLOTS * CHUNKS,)),
        ],
        compiler_params=pltpu.CompilerParams(
            collective_id=0, has_side_effects=True, vmem_limit_bytes=28 * 2**20
        ),
        cost_estimate=pl.CostEstimate(
            flops=2 * 10**9, bytes_accessed=20 * 2**20, transcendentals=0
        ),
    )(*[
        pltpu.with_memory_space_constraint(value, pltpu.HBM)
        for value in (counts, grid, margin, factor, local_inverse)
    ])


def update_kernel(
    margin_ref, sub_ref, live_ref, flipped_ref, alive_ref, local_ref, coupling_ref, diag_ref,
    ordered, rank_smem, stage, cross_out, cross_in, c_send, c_recv, k_send, k_recv,
):
    front = lax.axis_index("front")
    row = lax.axis_index("row")
    x, core = front // 2, front % 2
    z, y = row // 4, row % 4
    mine = (y * (1 - core) + z * core) % 2
    pair_up = partners(x, core, y, z, 1)
    pair_down = partners(x, core, y, z, 3)
    barrier = pltpu.get_barrier_semaphore()
    for other in (pair_up, pair_down):
        pl.semaphore_signal(barrier, inc=1, device_id=other, device_id_type=MESH)

    def rank(part, _):
        keys = [order(margin_ref[part, a]) for a in range(NOV)]
        for a in range(NOV):
            rank_smem[part, a] = sum((keys[b] < keys[a]).astype(jnp.int32) for b in range(NOV) if b != a)
        return 0


    totals = [jnp.zeros((256, 256), jnp.float32) for _ in range(2)]
    sends = []

    def block(a, b):
        return sub_ref[first_block(a) + b - a]

    def pair(index):
        a = 2 * index
        direct = jnp.concatenate(
            [
                jnp.concatenate([block(a, b) for b in range(a, NOV)], axis=1),
                jnp.concatenate(
                    [block(a, a + 1).T] + [block(a + 1, b) for b in range(a + 1, NOV)], axis=1
                ),
            ],
            axis=0,
        )
        result = jnp.dot(direct, live_ref[a * BLOCK :, :], preferred_element_type=jnp.float32)
        if index:
            mirrored = jnp.concatenate(
                [jnp.concatenate([block(b, a), block(b, a + 1)], axis=1) for b in range(a)], axis=0
            )
            turned = jnp.dot(
                flipped_ref[:, : a * BLOCK], mirrored, preferred_element_type=jnp.float32
            )
            result = result + turned.T
        halves = []
        for half in range(2):
            value = -result[half * BLOCK : (half + 1) * BLOCK]
            value = jnp.where(alive_ref[a + half, :1, :] > 0, value, jnp.zeros_like(value))
            halves.append(value.astype(jnp.bfloat16))
        return halves

    def send(source, target, send_sem, recv_sem, device):
        copy = pltpu.make_async_remote_copy(
            src_ref=source, dst_ref=target, send_sem=send_sem, recv_sem=recv_sem,
            device_id=device, device_id_type=MESH,
        )
        copy.start()
        sends.append(copy)

    def returned(part, first, number):
        return ordered.at[part, pl.ds(first, 4), :, pl.ds(number * BLOCK, BLOCK)]

    for index in range(8):
        rows = slice(2 * index * BLOCK, (2 * index + 2) * BLOCK)
        halves = pair(index)
        for half in range(2):
            ordered[mine, 2 * index + half] = halves[half][:, :256]
            stage[0, 2 * index + half] = halves[half][:, 256:384]
            stage[1, 2 * index + half] = halves[half][:, 384:]
        result = jnp.concatenate(halves, axis=0)
        for number in range(2):
            at = slice(256 * number, 256 * number + 256)
            totals[number] -= jnp.dot(
                flipped_ref[at, rows], result[:, at], preferred_element_type=jnp.float32
            )
        if index == 1:
            pl.semaphore_wait(barrier, 2)
        if index % 2:
            first = 2 * index - 2
            for number, device in enumerate((pair_down, pair_up)):
                slot = 2 * (index // 2) + number
                send(
                    stage.at[number, pl.ds(first, 4)], returned(mine, first, number),
                    c_send.at[slot], c_recv.at[slot], device,
                )

    for number, device in enumerate((pair_down, pair_up)):
        at = slice(number * BLOCK, (number + 1) * BLOCK)
        cross_out[number] = totals[1][at, at]
        send(
            cross_out.at[number], cross_in.at[number],
            k_send.at[number], k_recv.at[number], device,
        )
    for number in range(2):
        at = slice(number * BLOCK, (number + 1) * BLOCK)
        diag_ref[mine, number] = local_ref[mine, at, at] + totals[0][at, at]
    def restore(part):
        def one(a, _):
            rows = pl.multiple_of(a * BLOCK, BLOCK)
            coupling_ref[part, pl.ds(rows, BLOCK), :] = ordered[part, rank_smem[part, a]]
            return 0

        lax.fori_loop(0, NOV, one, 0)

    for number in range(2):
        at = slice(number * BLOCK, (number + 1) * BLOCK)
        pltpu.make_async_copy(cross_in.at[number], cross_in.at[number], k_recv.at[number]).wait()
        diag_ref[1 - mine, number] = local_ref[1 - mine, at, at] + cross_in[number]
    lax.fori_loop(0, 2, rank, 0)
    for quarter in range(4):
        for number in range(2):
            ref = returned(1 - mine, quarter * 4, number)
            pltpu.make_async_copy(ref, ref, c_recv.at[2 * quarter + number]).wait()
    restore(mine)
    restore(1 - mine)
    for copy in sends:
        copy.wait_send()


def body(parent, margin, counts, factor, local_inverse):
    sub, live, flipped, alive, local = gathered(parent, margin, counts, factor, local_inverse)
    vmem = pl.BlockSpec(memory_space=pltpu.VMEM)
    dma = pltpu.SemaphoreType.DMA
    return pl.pallas_call(
        update_kernel,
        out_shape=(
            jax.ShapeDtypeStruct(factor.shape, jnp.bfloat16),
            jax.ShapeDtypeStruct((2, 2, BLOCK, BLOCK), jnp.float32),
        ),
        in_specs=[pl.BlockSpec(memory_space=pltpu.SMEM)] + [vmem] * 5,
        out_specs=(vmem, vmem),
        scratch_shapes=[
            pltpu.VMEM((2, NOV, BLOCK, 256), jnp.bfloat16),
            pltpu.SMEM((2, NOV), jnp.int32),
            pltpu.VMEM((2, NOV, BLOCK, BLOCK), jnp.bfloat16),
            pltpu.VMEM((2, BLOCK, BLOCK), jnp.float32),
            pltpu.VMEM((2, BLOCK, BLOCK), jnp.float32),
            dma((8,)), dma((8,)), dma((2,)), dma((2,)),
        ],
        compiler_params=pltpu.CompilerParams(
            collective_id=1, has_side_effects=True, vmem_limit_bytes=24 * 2**20
        ),
        cost_estimate=pl.CostEstimate(
            flops=6 * 10**9, bytes_accessed=20 * 2**20, transcendentals=0
        ),
    )(margin, sub.reshape(BLOCKS, BLOCK, BLOCK), live, flipped, alive, local)


def solution(mesh):
    placed = (
        P(("front", "row"), None),
        P("front", None),
        P("front"),
        P("front", None, "row"),
        P("front", None, "row"),
    )
    return jax.shard_map(
        body,
        mesh=mesh,
        in_specs=placed,
        out_specs=(P("front", None, "row"), P("front", "row", None, None)),
        check_vma=False,
    )
```

```python
import functools

import jax
import jax.numpy as jnp
from jax import lax
from jax.experimental import pallas as pl
from jax.experimental.pallas import tpu as pltpu
from jax.sharding import PartitionSpec as P

MESH = pl.DeviceIdType.MESH
NOV = 16
BLOCK = 128
BLOCKS = 136
CUTS = (0, 3, 16)
CHUNKS = len(CUTS) - 1
SLOTS = 20


def place(x, core, y, z):
    return (2 * x + core, 4 * z + y)


def first_block(a):
    return NOV * a - a * (a - 1) // 2


def order(block):
    x, core, z, yh = block >> 4, (block >> 3) & 1, (block >> 1) & 3, block & 1
    group = z * (1 - core) + (7 - z) * core
    return group * 8 + x * 2 + yh


def network(count):
    swaps, p = [], 1
    while p < count:
        k = p
        while k >= 1:
            for j in range(k % p, count - k, 2 * k):
                for i in range(min(k, count - j - k)):
                    if (i + j) // (2 * p) == (i + j + k) // (2 * p):
                        swaps.append((i + j, i + j + k))
            k //= 2
        p *= 2
    return swaps


def columns(core, z):
    return (2 * z, 16 - 2 * z) if core == 0 else (8, 2 * z + 2)


def spans(chunk):
    first, last = first_block(CUTS[chunk]), first_block(CUTS[chunk + 1])
    return first, last - first


def partners(x, core, y, z, up):
    return place(x, core, (y + up * (1 - core)) % 4, (z + up * core) % 4)


def others(x, core, y, z, up):
    return place(x, core, (y + up * core) % 4, (z + up * (1 - core)) % 4)


def prepare_factor(
    count, part, ranked, factor_buf, lent_buf, live_ref, flipped_ref, alive_ref
):
    def mask(at, _):
        a = ranked(at)
        rows = pl.multiple_of(at * BLOCK, BLOCK)
        value = jnp.concatenate([factor_buf[part, a], lent_buf[0, a], lent_buf[1, a]], axis=1)
        value = jnp.where(a < count, value, jnp.zeros_like(value))
        live_ref[pl.ds(rows, BLOCK), :] = value
        flipped_ref[:, pl.ds(rows, BLOCK)] = value.T
        ones = jnp.ones((8, 512), jnp.float32)
        alive_ref[at] = jnp.where(a < count, ones, jnp.zeros_like(ones))
        return 0

    lax.fori_loop(0, NOV, mask, 0)


def prepare_local(part, first_col, inverse_buf, local_ref):
    def local(step, total):
        rows = pl.multiple_of(step * 512, 512)
        value = inverse_buf[part, pl.ds(rows, 512), :]
        row_at = rows + lax.broadcasted_iota(jnp.int32, value.shape, 0)
        col_at = first_col + lax.broadcasted_iota(jnp.int32, value.shape, 1)
        value = jnp.where(row_at >= col_at, value, jnp.zeros_like(value))
        return total + lax.dot_general(
            value, value, (((0,), (0,)), ((), ())), preferred_element_type=jnp.float32
        )

    local_ref[part] = lax.fori_loop(0, 8, local, jnp.zeros((256, 256), jnp.float32))


def gather_kernel(
    counts_ref, parent_ref, margin_ref, factor_ref, inverse_ref,
    out_ref, live_ref, flipped_ref, alive_ref, local_ref,
    parent_buf, factor_buf, inverse_buf, lent_buf, other_buf, slabs, picked, margin_buf, margin_smem, sorted_smem, ranked_smem, counts_smem,
    t_send, t_recv, d_send, d_recv, m_send, m_recv, l_sem, f_send, f_recv, x_send, x_recv, g_send, g_recv,
):
    front = lax.axis_index("front")
    row = lax.axis_index("row")
    x, core = front // 2, front % 2
    z, y = row // 4, row % 4
    half, yh = y % 2, y // 2
    fold = half * 2 + yh
    me_q = yh * 16 + z * 4 + x
    my_block = 16 * x + 8 * core + 2 * z + yh
    here = y * (1 - core) + z * core
    there = z * (1 - core) + y * core
    mine = here % 2
    sibling = place(x, 1 - core, y, z)
    pair_up = partners(x, core, y, z, 1)
    pair_down = partners(x, core, y, z, 3)
    pair_far = partners(x, core, y, z, 2)
    ring_up = others(x, core, y, z, 1)
    ring_down = others(x, core, y, z, 3)
    y_up = place(x, core, (y + 1) % 4, z)
    y_down = place(x, core, (y + 3) % 4, z)

    def member(q):
        return place(q % 4, core, 2 * (q // 16) + half, (q // 4) % 4)

    parent_load = pltpu.make_async_copy(parent_ref, parent_buf, l_sem.at[0])
    parent_load.start()
    factor_load = pltpu.make_async_copy(factor_ref, factor_buf, l_sem.at[1])
    factor_load.start()
    inverse_load = pltpu.make_async_copy(inverse_ref, inverse_buf, l_sem.at[2])
    inverse_load.start()
    counts_load = pltpu.make_async_copy(counts_ref, counts_smem, l_sem.at[4])
    counts_load.start()

    barrier = pltpu.get_barrier_semaphore()

    def greet(step, _):
        pl.semaphore_signal(
            barrier, inc=1, device_id=member((me_q + step) % 32), device_id_type=MESH
        )
        return 0

    lax.fori_loop(1, 32, greet, 0)
    for other in (sibling, y_up, y_down):
        pl.semaphore_signal(barrier, inc=1, device_id=other, device_id_type=MESH)
    parent_load.wait()
    pl.semaphore_wait(barrier, 34)

    margin_sends = []
    for step in (1, 2, 3):
        copy = pltpu.make_async_remote_copy(
            src_ref=margin_ref,
            dst_ref=margin_buf.at[x],
            send_sem=m_send.at[step],
            recv_sem=m_recv.at[x],
            device_id=place((x + step) % 4, core, y, z),
            device_id_type=MESH,
        )
        copy.start()
        margin_sends.append(copy)
    pltpu.make_async_copy(margin_ref, margin_buf.at[x], m_recv.at[x]).start()

    def spread_all(own_core, own_z):
        cols = pl.ds(*columns(own_core, own_z))
        pltpu.make_async_copy(
            parent_buf.at[me_q // 4, :, cols, me_q % 4],
            slabs.at[my_block, :, cols],
            t_recv.at[x],
        ).start()
        for offset in (0, 1, 3, 2):

            def spread(step, _):
                q = (yh * 4 + z + step) % 8 * 4 + (x + offset) % 4
                pltpu.make_async_remote_copy(
                    src_ref=parent_buf.at[q // 4, :, cols, q % 4],
                    dst_ref=slabs.at[my_block, :, cols],
                    send_sem=t_send,
                    recv_sem=t_recv.at[x],
                    device_id=member(q),
                    device_id_type=MESH,
                ).start()
                return 0

            lax.fori_loop(0 if offset else 1, 8, spread, 0)

    for own_core in range(2):
        for own_z in range(4):
            pl.when(jnp.logical_and(core == own_core, z == own_z))(
                functools.partial(spread_all, own_core, own_z)
            )

    for source in range(4):
        pltpu.make_async_copy(margin_ref, margin_buf.at[source], m_recv.at[source]).wait()
    to_smem = pltpu.make_async_copy(margin_buf, margin_smem, l_sem.at[3])
    to_smem.start()
    to_smem.wait()

    swaps = network(NOV)

    def sort(index, _):
        target, part = index // 2, index % 2
        keys = []
        for a in range(NOV):
            block = margin_smem[target, part, a]
            keys.append(order(block) * 1024 + block * NOV + a)
        for i, j in swaps:
            keys[i], keys[j] = jnp.minimum(keys[i], keys[j]), jnp.maximum(keys[i], keys[j])
        for a in range(NOV):
            sorted_smem[target, part, a] = (keys[a] >> 4) & 63
            ranked_smem[target, part, a] = keys[a] & (NOV - 1)
        return 0

    lax.fori_loop(0, 8, sort, 0)

    def swap_cores(own_core, wait_only):
        total = sum(columns(own_core, own_z)[1] for own_z in range(4)) // 4
        for offset in (0, 1, 3, 2):
            source = (x + 4 - offset) % 4
            if not wait_only:
                group = slabs.at[pl.ds(0, 8), :, pl.ds(0, total)]
                pltpu.make_async_copy(group, group, t_recv.at[source]).wait()
            for own_z in range(4):
                part = slabs.at[
                    pl.ds(16 * source + 8 * own_core + 2 * own_z, 2), :,
                    pl.ds(*columns(own_core, own_z)),
                ]
                slot = 4 * source + own_z
                if wait_only:
                    pltpu.make_async_copy(part, part, d_recv.at[slot]).wait()
                else:
                    pltpu.make_async_remote_copy(
                        src_ref=part,
                        dst_ref=part,
                        send_sem=d_send.at[slot],
                        recv_sem=d_recv.at[slot],
                        device_id=sibling,
                        device_id_type=MESH,
                    ).start()

    def swap_sent(own_core):
        for source in range(4):
            for own_z in range(4):
                part = slabs.at[
                    pl.ds(16 * source + 8 * own_core + 2 * own_z, 2), :,
                    pl.ds(*columns(own_core, own_z)),
                ]
                pltpu.make_async_copy(part, part, d_send.at[4 * source + own_z]).wait()

    for own_core in range(2):
        pl.when(core == own_core)(functools.partial(swap_cores, own_core, False))

    factor_load.wait()
    lends = []
    for number, device in enumerate((pair_up, pair_down)):
        copy = pltpu.make_async_remote_copy(
            src_ref=factor_buf.at[1 - mine, :, :, pl.ds(number * BLOCK, BLOCK)],
            dst_ref=lent_buf.at[number],
            send_sem=f_send.at[number],
            recv_sem=f_recv.at[number],
            device_id=device,
            device_id_type=MESH,
        )
        copy.start()
        lends.append(copy)

    for own_core in range(2):
        pl.when(core == 1 - own_core)(functools.partial(swap_cores, own_core, True))

    x_copies = [[] for _ in range(CHUNKS)]

    def start_x(chunk):
        blocks = pl.ds(*spans(chunk))
        for step in (2, 1, 3, 0):
            target = (x + step) % 4

            def pick(part, _):
                ids = [sorted_smem[target, part, a] for a in range(NOV)]
                for a in range(CUTS[chunk], CUTS[chunk + 1]):
                    for b in range(a, NOV):
                        block = slabs[ids[a], ids[b] >> 4, ids[b] & 15]
                        picked[target, part, first_block(a) + b - a] = block
                return 0

            lax.fori_loop(0, 2, pick, 0)
            slot = 8 * chunk + 2 * step
            lands = (out_ref.at[blocks, fold, z, x], other_buf.at[blocks, x])
            for number, land in enumerate(lands):
                part = (mine + number) % 2
                if step:
                    copy = pltpu.make_async_remote_copy(
                        src_ref=picked.at[target, part, blocks],
                        dst_ref=land,
                        send_sem=x_send.at[slot + number],
                        recv_sem=x_recv.at[slot + number],
                        device_id=place(target, core, y, z),
                        device_id_type=MESH,
                    )
                else:
                    copy = pltpu.make_async_copy(
                        picked.at[target, part, blocks], land, x_recv.at[slot + number]
                    )
                copy.start()
                x_copies[chunk].append(copy)

    sends = []

    def piece(chunk, pair_at, ring_at, side=None):
        y_at = pair_at * (1 - core) + ring_at * core
        z_at = ring_at * (1 - core) + pair_at * core
        first, count = spans(chunk)
        if side == 0:
            count = count // 2
        if side == 1:
            first, count = first + count // 2, count - count // 2
        return out_ref.at[pl.ds(first, count), (y_at % 2) * 2 + y_at // 2, z_at]

    def send(chunk, slot, source, target, device):
        at = SLOTS * chunk + slot
        copy = pltpu.make_async_remote_copy(
            src_ref=source, dst_ref=target, send_sem=g_send.at[at], recv_sem=g_recv.at[at],
            device_id=device, device_id_type=MESH,
        )
        copy.start()
        sends.append(copy)

    def landed(chunk, slot, ref):
        pltpu.make_async_copy(ref, ref, g_recv.at[SLOTS * chunk + slot]).wait()

    pair_places = (here, (here + 3) % 4, (here + 1) % 4, (here + 2) % 4)
    above, below, far = (there + 1) % 4, (there + 3) % 4, (there + 2) % 4

    def ring_direct(chunk, number):
        own = piece(chunk, pair_places[number], there)
        send(chunk, 4 + 4 * number, own, own, ring_up)
        send(chunk, 5 + 4 * number, own, own, ring_down)

    def ring_forward(chunk, number):
        at = pair_places[number]
        landed(chunk, 4 + 4 * number, piece(chunk, at, below))
        low = piece(chunk, at, below, 0)
        send(chunk, 6 + 4 * number, low, low, ring_up)
        landed(chunk, 5 + 4 * number, piece(chunk, at, above))
        high = piece(chunk, at, above, 1)
        send(chunk, 7 + 4 * number, high, high, ring_down)

    def step_own(chunk):
        for copy in x_copies[chunk]:
            copy.wait()
        own = piece(chunk, here, there)
        other = other_buf.at[pl.ds(*spans(chunk))]
        send(chunk, 0, other, own, pair_up)
        send(chunk, 1, other, own, pair_down)
        send(chunk, 2, own, own, pair_far)
        ring_direct(chunk, 0)

    def step_near(chunk):
        for number in (1, 2, 3):
            landed(chunk, number - 1, piece(chunk, pair_places[number], there))
            ring_direct(chunk, number)
        ring_forward(chunk, 0)

    def step_far(chunk):
        for number in (1, 2, 3):
            ring_forward(chunk, number)

    def step_end(chunk):
        for number, at in enumerate(pair_places):
            landed(chunk, 6 + 4 * number, piece(chunk, at, far, 0))
            landed(chunk, 7 + 4 * number, piece(chunk, at, far, 1))

    start_x(0)
    start_x(1)
    for turn in range(CHUNKS + 3):
        for delay, step in enumerate((step_own, step_near, step_far, step_end)):
            if 0 <= turn - delay < CHUNKS:
                step(turn - delay)
                if delay == 0 and turn + 2 < CHUNKS:
                    start_x(turn + 2)
        if turn == min(1, CHUNKS - 1):
            for copy in lends:
                copy.wait()
            counts_load.wait()
            prepare_factor(
                counts_smem[mine], mine, lambda at: ranked_smem[x, mine, at],
                factor_buf, lent_buf, live_ref, flipped_ref, alive_ref,
            )
        if turn == min(2, CHUNKS):
            inverse_load.wait()
            for part in range(2):
                prepare_local(part, row * 256, inverse_buf, local_ref)

    for copy in sends:
        copy.wait_send()
    for copy in margin_sends:
        copy.wait_send()

    def spread_sent(own_core, own_z):
        sent = slabs.at[pl.ds(0, 31), :, pl.ds(0, columns(own_core, own_z)[1])]
        pltpu.make_async_copy(sent, sent, t_send).wait()

    for own_core in range(2):
        pl.when(core == own_core)(functools.partial(swap_sent, own_core))
        for own_z in range(4):
            pl.when(jnp.logical_and(core == own_core, z == own_z))(
                functools.partial(spread_sent, own_core, own_z)
            )


def gathered(parent, margin, counts, factor, local_inverse):
    grid = parent.reshape(8, 4, 2, 4, 16, BLOCK).transpose(0, 3, 4, 1, 2, 5)
    factor = factor.reshape(2, NOV, BLOCK, 256)
    dma = pltpu.SemaphoreType.DMA
    vmem = pl.BlockSpec(memory_space=pltpu.VMEM)
    hbm = pl.BlockSpec(memory_space=pltpu.HBM)
    return pl.pallas_call(
        gather_kernel,
        out_shape=(
            jax.ShapeDtypeStruct((BLOCKS, 4, 4, 4, 2, BLOCK), jnp.bfloat16),
            jax.ShapeDtypeStruct((2048, 512), jnp.bfloat16),
            jax.ShapeDtypeStruct((512, 2048), jnp.bfloat16),
            jax.ShapeDtypeStruct((NOV, 8, 512), jnp.float32),
            jax.ShapeDtypeStruct((2, 256, 256), jnp.float32),
        ),
        in_specs=[hbm] * 5,
        out_specs=(vmem,) * 5,
        scratch_shapes=[
            pltpu.VMEM(grid.shape, jnp.bfloat16),
            pltpu.VMEM(factor.shape, jnp.bfloat16),
            pltpu.VMEM(local_inverse.shape, jnp.bfloat16),
            pltpu.VMEM((2, NOV, BLOCK, BLOCK), jnp.bfloat16),
            pltpu.VMEM((BLOCKS, 4, 2, BLOCK), jnp.bfloat16),
            pltpu.VMEM((64, 4, 16, 2, BLOCK), jnp.bfloat16),
            pltpu.VMEM((4, 2, BLOCKS, 2, BLOCK), jnp.bfloat16),
            pltpu.VMEM((4, 2, NOV), jnp.int32),
            pltpu.SMEM((4, 2, NOV), jnp.int32),
            pltpu.SMEM((4, 2, NOV), jnp.int32),
            pltpu.SMEM((4, 2, NOV), jnp.int32),
            pltpu.SMEM((2,), jnp.int32),
            dma, dma((4,)), dma((16,)), dma((16,)), dma((4,)), dma((4,)), dma((5,)),
            dma((2,)), dma((2,)), dma((8 * CHUNKS,)), dma((8 * CHUNKS,)),
            dma((SLOTS * CHUNKS,)), dma((SLOTS * CHUNKS,)),
        ],
        compiler_params=pltpu.CompilerParams(
            collective_id=0, has_side_effects=True, vmem_limit_bytes=28 * 2**20
        ),
        cost_estimate=pl.CostEstimate(
            flops=2 * 10**9, bytes_accessed=20 * 2**20, transcendentals=0
        ),
    )(*[
        pltpu.with_memory_space_constraint(value, pltpu.HBM)
        for value in (counts, grid, margin, factor, local_inverse)
    ])


def update_kernel(
    margin_ref, sub_ref, live_ref, flipped_ref, alive_ref, local_ref, coupling_ref, diag_ref,
    ordered, rank_smem, stage, cross_out, cross_in, c_send, c_recv, k_send, k_recv,
):
    front = lax.axis_index("front")
    row = lax.axis_index("row")
    x, core = front // 2, front % 2
    z, y = row // 4, row % 4
    mine = (y * (1 - core) + z * core) % 2
    pair_up = partners(x, core, y, z, 1)
    pair_down = partners(x, core, y, z, 3)
    barrier = pltpu.get_barrier_semaphore()
    for other in (pair_up, pair_down):
        pl.semaphore_signal(barrier, inc=1, device_id=other, device_id_type=MESH)

    def rank(part, _):
        keys = [order(margin_ref[part, a]) for a in range(NOV)]
        for a in range(NOV):
            rank_smem[part, a] = sum((keys[b] < keys[a]).astype(jnp.int32) for b in range(NOV) if b != a)
        return 0


    sends = []

    def block(a, b):
        return sub_ref[first_block(a) + b - a]

    def pair(index, cols):
        a = 2 * index
        direct = jnp.concatenate(
            [
                jnp.concatenate([block(a, b) for b in range(a, NOV)], axis=1),
                jnp.concatenate(
                    [block(a, a + 1).T] + [block(a + 1, b) for b in range(a + 1, NOV)], axis=1
                ),
            ],
            axis=0,
        )
        result = jnp.dot(direct, live_ref[a * BLOCK :, cols], preferred_element_type=jnp.float32)
        if index:
            mirrored = jnp.concatenate(
                [jnp.concatenate([block(b, a), block(b, a + 1)], axis=1) for b in range(a)], axis=0
            )
            turned = jnp.dot(
                flipped_ref[cols, : a * BLOCK], mirrored, preferred_element_type=jnp.float32
            )
            result = result + turned.T
        halves = []
        for half in range(2):
            value = -result[half * BLOCK : (half + 1) * BLOCK]
            value = jnp.where(alive_ref[a + half, :1, : cols.stop - cols.start] > 0, value, jnp.zeros_like(value))
            halves.append(value.astype(jnp.bfloat16))
        return halves

    def send(source, target, send_sem, recv_sem, device):
        copy = pltpu.make_async_remote_copy(
            src_ref=source, dst_ref=target, send_sem=send_sem, recv_sem=recv_sem,
            device_id=device, device_id_type=MESH,
        )
        copy.start()
        sends.append(copy)

    def returned(part, first, number):
        return ordered.at[part, pl.ds(first, 4), :, pl.ds(number * BLOCK, BLOCK)]

    def cross(cols, value):
        return jnp.dot(
            flipped_ref[cols, :], value.reshape(NOV * BLOCK, 256),
            preferred_element_type=jnp.float32,
        )

    own, lent, both = slice(0, 256), slice(256, 512), slice(0, 512)
    for part in range(2):
        rank(part, 0)
    order_of_work = [(index, both) for index in range(4)]
    order_of_work += [(index, lent) for index in range(4, 8)]
    order_of_work += [(index, own) for index in range(4, 8)]
    for index, cols in order_of_work:
        halves = pair(index, cols)
        for half in range(2):
            at = 2 * index + half
            if cols is not lent:
                ordered[mine, at] = halves[half][:, :256]
            if cols is not own:
                stage[0, at] = halves[half][:, -256:-128]
                stage[1, at] = halves[half][:, -128:]
        if cols is own:
            continue
        if index == 1:
            pl.semaphore_wait(barrier, 2)
        if index % 2 == 2 - 1 and index:
            for done in (0, 1) if index == 1 and 2 == 1 else (index // 2,):
                for number, device in enumerate((pair_down, pair_up)):
                    slot = 2 * done + number
                    send(
                        stage.at[number, pl.ds(4 * done, 4)],
                        returned(mine, 4 * done, number),
                        c_send.at[slot], c_recv.at[slot], device,
                    )
        if index == 7:
            total = cross(lent, jnp.concatenate([stage[0], stage[1]], axis=2))
            for number, device in enumerate((pair_down, pair_up)):
                at = slice(number * BLOCK, (number + 1) * BLOCK)
                cross_out[number] = -total[at, at]
                send(
                    cross_out.at[number], cross_in.at[number],
                    k_send.at[number], k_recv.at[number], device,
                )
    total = cross(own, ordered[mine])

    for number in range(2):
        at = slice(number * BLOCK, (number + 1) * BLOCK)
        diag_ref[mine, number] = local_ref[mine, at, at] - total[at, at]
    def restore(part):
        def one(a, _):
            rows = pl.multiple_of(a * BLOCK, BLOCK)
            coupling_ref[part, pl.ds(rows, BLOCK), :] = ordered[part, rank_smem[part, a]]
            return 0

        lax.fori_loop(0, NOV, one, 0, unroll=4)

    for number in range(2):
        at = slice(number * BLOCK, (number + 1) * BLOCK)
        pltpu.make_async_copy(cross_in.at[number], cross_in.at[number], k_recv.at[number]).wait()
        diag_ref[1 - mine, number] = local_ref[1 - mine, at, at] + cross_in[number]
    for quarter in range(4):
        for number in range(2):
            ref = returned(1 - mine, quarter * 4, number)
            pltpu.make_async_copy(ref, ref, c_recv.at[2 * quarter + number]).wait()
    restore(mine)
    restore(1 - mine)
    for copy in sends:
        copy.wait_send()


def body(parent, margin, counts, factor, local_inverse):
    sub, live, flipped, alive, local = gathered(parent, margin, counts, factor, local_inverse)
    vmem = pl.BlockSpec(memory_space=pltpu.VMEM)
    dma = pltpu.SemaphoreType.DMA
    return pl.pallas_call(
        update_kernel,
        out_shape=(
            jax.ShapeDtypeStruct(factor.shape, jnp.bfloat16),
            jax.ShapeDtypeStruct((2, 2, BLOCK, BLOCK), jnp.float32),
        ),
        in_specs=[pl.BlockSpec(memory_space=pltpu.SMEM)] + [vmem] * 5,
        out_specs=(vmem, vmem),
        scratch_shapes=[
            pltpu.VMEM((2, NOV, BLOCK, 256), jnp.bfloat16),
            pltpu.SMEM((2, NOV), jnp.int32),
            pltpu.VMEM((2, NOV, BLOCK, BLOCK), jnp.bfloat16),
            pltpu.VMEM((2, BLOCK, BLOCK), jnp.float32),
            pltpu.VMEM((2, BLOCK, BLOCK), jnp.float32),
            dma((8,)), dma((8,)), dma((2,)), dma((2,)),
        ],
        compiler_params=pltpu.CompilerParams(
            collective_id=1, has_side_effects=True, vmem_limit_bytes=24 * 2**20
        ),
        cost_estimate=pl.CostEstimate(
            flops=6 * 10**9, bytes_accessed=20 * 2**20, transcendentals=0
        ),
    )(margin, sub.reshape(BLOCKS, BLOCK, BLOCK), live, flipped, alive, local)


def solution(mesh):
    placed = (
        P(("front", "row"), None),
        P("front", None),
        P("front"),
        P("front", None, "row"),
        P("front", None, "row"),
    )
    return jax.shard_map(
        body,
        mesh=mesh,
        in_specs=placed,
        out_specs=(P("front", None, "row"), P("front", "row", None, None)),
        check_vma=False,
    )
```

```python
import functools

import jax
import jax.numpy as jnp
from jax import lax
from jax.experimental import pallas as pl
from jax.experimental.pallas import tpu as pltpu
from jax.sharding import PartitionSpec as P

MESH = pl.DeviceIdType.MESH
NOV = 16
BLOCK = 128
BLOCKS = 136
CUTS = (0, 2, 6, 16)
CHUNKS = len(CUTS) - 1
SLOTS = 20


def place(x, core, y, z):
    return (2 * x + core, 4 * z + y)


def first_block(a):
    return NOV * a - a * (a - 1) // 2


def order(block):
    x, core, z, yh = block >> 4, (block >> 3) & 1, (block >> 1) & 3, block & 1
    group = z * (1 - core) + (7 - z) * core
    return group * 8 + x * 2 + yh


def network(count):
    swaps, p = [], 1
    while p < count:
        k = p
        while k >= 1:
            for j in range(k % p, count - k, 2 * k):
                for i in range(min(k, count - j - k)):
                    if (i + j) // (2 * p) == (i + j + k) // (2 * p):
                        swaps.append((i + j, i + j + k))
            k //= 2
        p *= 2
    return swaps


def columns(core, z):
    return (2 * z, 16 - 2 * z) if core == 0 else (8, 2 * z + 2)


def spans(chunk):
    first, last = first_block(CUTS[chunk]), first_block(CUTS[chunk + 1])
    return first, last - first


def partners(x, core, y, z, up):
    return place(x, core, (y + up * (1 - core)) % 4, (z + up * core) % 4)


def others(x, core, y, z, up):
    return place(x, core, (y + up * core) % 4, (z + up * (1 - core)) % 4)


def prepare_factor(
    count, part, ranked, factor_buf, lent_buf, live_ref, flipped_ref, alive_ref
):
    def mask(at, _):
        a = ranked(at)
        rows = pl.multiple_of(at * BLOCK, BLOCK)
        value = jnp.concatenate([factor_buf[part, a], lent_buf[0, a], lent_buf[1, a]], axis=1)
        value = jnp.where(a < count, value, jnp.zeros_like(value))
        live_ref[pl.ds(rows, BLOCK), :] = value
        flipped_ref[:, pl.ds(rows, BLOCK)] = value.T
        ones = jnp.ones((8, 512), jnp.float32)
        alive_ref[at] = jnp.where(a < count, ones, jnp.zeros_like(ones))
        return 0

    lax.fori_loop(0, NOV, mask, 0)


def prepare_local(part, first_col, inverse_buf, local_ref):
    def local(step, total):
        rows = pl.multiple_of(step * 512, 512)
        value = inverse_buf[part, pl.ds(rows, 512), :]
        row_at = rows + lax.broadcasted_iota(jnp.int32, value.shape, 0)
        col_at = first_col + lax.broadcasted_iota(jnp.int32, value.shape, 1)
        value = jnp.where(row_at >= col_at, value, jnp.zeros_like(value))
        return total + lax.dot_general(
            value, value, (((0,), (0,)), ((), ())), preferred_element_type=jnp.float32
        )

    local_ref[part] = lax.fori_loop(0, 8, local, jnp.zeros((256, 256), jnp.float32))


def gather_kernel(
    counts_ref, parent_ref, margin_ref, factor_ref, inverse_ref,
    out_ref, live_ref, flipped_ref, alive_ref, local_ref,
    parent_buf, factor_buf, inverse_buf, lent_buf, other_buf, slabs, picked, margin_buf, margin_smem, sorted_smem, ranked_smem, counts_smem,
    t_send, t_recv, d_send, d_recv, m_send, m_recv, l_sem, f_send, f_recv, x_send, x_recv, g_send, g_recv,
):
    front = lax.axis_index("front")
    row = lax.axis_index("row")
    x, core = front // 2, front % 2
    z, y = row // 4, row % 4
    half, yh = y % 2, y // 2
    fold = half * 2 + yh
    me_q = yh * 16 + z * 4 + x
    my_block = 16 * x + 8 * core + 2 * z + yh
    here = y * (1 - core) + z * core
    there = z * (1 - core) + y * core
    mine = here % 2
    sibling = place(x, 1 - core, y, z)
    pair_up = partners(x, core, y, z, 1)
    pair_down = partners(x, core, y, z, 3)
    pair_far = partners(x, core, y, z, 2)
    ring_up = others(x, core, y, z, 1)
    ring_down = others(x, core, y, z, 3)
    y_up = place(x, core, (y + 1) % 4, z)
    y_down = place(x, core, (y + 3) % 4, z)

    def member(q):
        return place(q % 4, core, 2 * (q // 16) + half, (q // 4) % 4)

    parent_load = pltpu.make_async_copy(parent_ref, parent_buf, l_sem.at[0])
    parent_load.start()
    factor_load = pltpu.make_async_copy(factor_ref, factor_buf, l_sem.at[1])
    factor_load.start()
    inverse_load = pltpu.make_async_copy(inverse_ref, inverse_buf, l_sem.at[2])
    inverse_load.start()
    counts_load = pltpu.make_async_copy(counts_ref, counts_smem, l_sem.at[4])
    counts_load.start()

    barrier = pltpu.get_barrier_semaphore()

    def greet(step, _):
        pl.semaphore_signal(
            barrier, inc=1, device_id=member((me_q + step) % 32), device_id_type=MESH
        )
        return 0

    lax.fori_loop(1, 32, greet, 0)
    for other in (sibling, y_up, y_down):
        pl.semaphore_signal(barrier, inc=1, device_id=other, device_id_type=MESH)
    parent_load.wait()
    pl.semaphore_wait(barrier, 34)

    margin_sends = []
    for step in (1, 2, 3):
        copy = pltpu.make_async_remote_copy(
            src_ref=margin_ref,
            dst_ref=margin_buf.at[x],
            send_sem=m_send.at[step],
            recv_sem=m_recv.at[x],
            device_id=place((x + step) % 4, core, y, z),
            device_id_type=MESH,
        )
        copy.start()
        margin_sends.append(copy)
    pltpu.make_async_copy(margin_ref, margin_buf.at[x], m_recv.at[x]).start()

    def spread_all(own_core, own_z):
        cols = pl.ds(*columns(own_core, own_z))
        pltpu.make_async_copy(
            parent_buf.at[me_q // 4, :, cols, me_q % 4],
            slabs.at[my_block, :, cols],
            t_recv.at[x],
        ).start()
        for offset in (0, 1, 3, 2):

            def spread(step, _):
                q = (yh * 4 + z + step) % 8 * 4 + (x + offset) % 4
                pltpu.make_async_remote_copy(
                    src_ref=parent_buf.at[q // 4, :, cols, q % 4],
                    dst_ref=slabs.at[my_block, :, cols],
                    send_sem=t_send,
                    recv_sem=t_recv.at[x],
                    device_id=member(q),
                    device_id_type=MESH,
                ).start()
                return 0

            lax.fori_loop(0 if offset else 1, 8, spread, 0)

    for own_core in range(2):
        for own_z in range(4):
            pl.when(jnp.logical_and(core == own_core, z == own_z))(
                functools.partial(spread_all, own_core, own_z)
            )

    for source in range(4):
        pltpu.make_async_copy(margin_ref, margin_buf.at[source], m_recv.at[source]).wait()
    to_smem = pltpu.make_async_copy(margin_buf, margin_smem, l_sem.at[3])
    to_smem.start()
    to_smem.wait()

    swaps = network(NOV)

    def sort(index, _):
        target, part = index // 2, index % 2
        keys = []
        for a in range(NOV):
            block = margin_smem[target, part, a]
            keys.append(order(block) * 1024 + block * NOV + a)
        for i, j in swaps:
            keys[i], keys[j] = jnp.minimum(keys[i], keys[j]), jnp.maximum(keys[i], keys[j])
        for a in range(NOV):
            sorted_smem[target, part, a] = (keys[a] >> 4) & 63
            ranked_smem[target, part, a] = keys[a] & (NOV - 1)
        return 0

    lax.fori_loop(0, 8, sort, 0)

    def swap_cores(own_core, wait_only):
        total = sum(columns(own_core, own_z)[1] for own_z in range(4)) // 4
        for offset in (0, 1, 3, 2):
            source = (x + 4 - offset) % 4
            if not wait_only:
                group = slabs.at[pl.ds(0, 8), :, pl.ds(0, total)]
                pltpu.make_async_copy(group, group, t_recv.at[source]).wait()
            for own_z in range(4):
                part = slabs.at[
                    pl.ds(16 * source + 8 * own_core + 2 * own_z, 2), :,
                    pl.ds(*columns(own_core, own_z)),
                ]
                slot = 4 * source + own_z
                if wait_only:
                    pltpu.make_async_copy(part, part, d_recv.at[slot]).wait()
                else:
                    pltpu.make_async_remote_copy(
                        src_ref=part,
                        dst_ref=part,
                        send_sem=d_send.at[slot],
                        recv_sem=d_recv.at[slot],
                        device_id=sibling,
                        device_id_type=MESH,
                    ).start()

    def swap_sent(own_core):
        for source in range(4):
            for own_z in range(4):
                part = slabs.at[
                    pl.ds(16 * source + 8 * own_core + 2 * own_z, 2), :,
                    pl.ds(*columns(own_core, own_z)),
                ]
                pltpu.make_async_copy(part, part, d_send.at[4 * source + own_z]).wait()

    for own_core in range(2):
        pl.when(core == own_core)(functools.partial(swap_cores, own_core, False))

    factor_load.wait()
    lends = []
    for number, device in enumerate((pair_up, pair_down)):
        copy = pltpu.make_async_remote_copy(
            src_ref=factor_buf.at[1 - mine, :, :, pl.ds(number * BLOCK, BLOCK)],
            dst_ref=lent_buf.at[number],
            send_sem=f_send.at[number],
            recv_sem=f_recv.at[number],
            device_id=device,
            device_id_type=MESH,
        )
        copy.start()
        lends.append(copy)

    for own_core in range(2):
        pl.when(core == 1 - own_core)(functools.partial(swap_cores, own_core, True))

    x_copies = [[] for _ in range(CHUNKS)]

    def start_x(chunk):
        blocks = pl.ds(*spans(chunk))
        for step in (2, 1, 3, 0):
            target = (x + step) % 4

            def pick(part, _):
                ids = [sorted_smem[target, part, a] for a in range(NOV)]
                for a in range(CUTS[chunk], CUTS[chunk + 1]):
                    for b in range(a, NOV):
                        block = slabs[ids[a], ids[b] >> 4, ids[b] & 15]
                        picked[target, part, first_block(a) + b - a] = block
                return 0

            lax.fori_loop(0, 2, pick, 0)
            slot = 8 * chunk + 2 * step
            lands = (out_ref.at[blocks, fold, z, x], other_buf.at[blocks, x])
            for number, land in enumerate(lands):
                part = (mine + number) % 2
                if step:
                    copy = pltpu.make_async_remote_copy(
                        src_ref=picked.at[target, part, blocks],
                        dst_ref=land,
                        send_sem=x_send.at[slot + number],
                        recv_sem=x_recv.at[slot + number],
                        device_id=place(target, core, y, z),
                        device_id_type=MESH,
                    )
                else:
                    copy = pltpu.make_async_copy(
                        picked.at[target, part, blocks], land, x_recv.at[slot + number]
                    )
                copy.start()
                x_copies[chunk].append(copy)

    sends = []

    def piece(chunk, pair_at, ring_at, side=None):
        y_at = pair_at * (1 - core) + ring_at * core
        z_at = ring_at * (1 - core) + pair_at * core
        first, count = spans(chunk)
        if side == 0:
            count = count // 2
        if side == 1:
            first, count = first + count // 2, count - count // 2
        return out_ref.at[pl.ds(first, count), (y_at % 2) * 2 + y_at // 2, z_at]

    def send(chunk, slot, source, target, device):
        at = SLOTS * chunk + slot
        copy = pltpu.make_async_remote_copy(
            src_ref=source, dst_ref=target, send_sem=g_send.at[at], recv_sem=g_recv.at[at],
            device_id=device, device_id_type=MESH,
        )
        copy.start()
        sends.append(copy)

    def landed(chunk, slot, ref):
        pltpu.make_async_copy(ref, ref, g_recv.at[SLOTS * chunk + slot]).wait()

    pair_places = (here, (here + 3) % 4, (here + 1) % 4, (here + 2) % 4)
    above, below, far = (there + 1) % 4, (there + 3) % 4, (there + 2) % 4

    def ring_direct(chunk, number):
        own = piece(chunk, pair_places[number], there)
        send(chunk, 4 + 4 * number, own, own, ring_up)
        send(chunk, 5 + 4 * number, own, own, ring_down)

    def ring_forward(chunk, number):
        at = pair_places[number]
        landed(chunk, 4 + 4 * number, piece(chunk, at, below))
        low = piece(chunk, at, below, 0)
        send(chunk, 6 + 4 * number, low, low, ring_up)
        landed(chunk, 5 + 4 * number, piece(chunk, at, above))
        high = piece(chunk, at, above, 1)
        send(chunk, 7 + 4 * number, high, high, ring_down)

    def step_own(chunk):
        for copy in x_copies[chunk]:
            copy.wait()
        own = piece(chunk, here, there)
        other = other_buf.at[pl.ds(*spans(chunk))]
        send(chunk, 0, other, own, pair_up)
        send(chunk, 1, other, own, pair_down)
        send(chunk, 2, own, own, pair_far)
        ring_direct(chunk, 0)

    def step_near(chunk):
        for number in (1, 2, 3):
            landed(chunk, number - 1, piece(chunk, pair_places[number], there))
            ring_direct(chunk, number)
        ring_forward(chunk, 0)

    def step_far(chunk):
        for number in (1, 2, 3):
            ring_forward(chunk, number)

    def step_end(chunk):
        for number, at in enumerate(pair_places):
            landed(chunk, 6 + 4 * number, piece(chunk, at, far, 0))
            landed(chunk, 7 + 4 * number, piece(chunk, at, far, 1))

    start_x(0)
    start_x(1)
    for turn in range(CHUNKS + 3):
        for delay, step in enumerate((step_own, step_near, step_far, step_end)):
            if 0 <= turn - delay < CHUNKS:
                step(turn - delay)
                if delay == 0 and turn + 2 < CHUNKS:
                    start_x(turn + 2)
        if turn == min(1, CHUNKS - 1):
            for copy in lends:
                copy.wait()
            counts_load.wait()
            prepare_factor(
                counts_smem[mine], mine, lambda at: ranked_smem[x, mine, at],
                factor_buf, lent_buf, live_ref, flipped_ref, alive_ref,
            )
        if turn == min(2, CHUNKS):
            inverse_load.wait()
            for part in range(2):
                prepare_local(part, row * 256, inverse_buf, local_ref)

    for copy in sends:
        copy.wait_send()
    for copy in margin_sends:
        copy.wait_send()

    def spread_sent(own_core, own_z):
        sent = slabs.at[pl.ds(0, 31), :, pl.ds(0, columns(own_core, own_z)[1])]
        pltpu.make_async_copy(sent, sent, t_send).wait()

    for own_core in range(2):
        pl.when(core == own_core)(functools.partial(swap_sent, own_core))
        for own_z in range(4):
            pl.when(jnp.logical_and(core == own_core, z == own_z))(
                functools.partial(spread_sent, own_core, own_z)
            )


def gathered(parent, margin, counts, factor, local_inverse):
    grid = parent.reshape(8, 4, 2, 4, 16, BLOCK).transpose(0, 3, 4, 1, 2, 5)
    factor = factor.reshape(2, NOV, BLOCK, 256)
    dma = pltpu.SemaphoreType.DMA
    vmem = pl.BlockSpec(memory_space=pltpu.VMEM)
    hbm = pl.BlockSpec(memory_space=pltpu.HBM)
    return pl.pallas_call(
        gather_kernel,
        out_shape=(
            jax.ShapeDtypeStruct((BLOCKS, 4, 4, 4, 2, BLOCK), jnp.bfloat16),
            jax.ShapeDtypeStruct((2048, 512), jnp.bfloat16),
            jax.ShapeDtypeStruct((512, 2048), jnp.bfloat16),
            jax.ShapeDtypeStruct((NOV, 8, 512), jnp.float32),
            jax.ShapeDtypeStruct((2, 256, 256), jnp.float32),
        ),
        in_specs=[hbm] * 5,
        out_specs=(vmem,) * 5,
        scratch_shapes=[
            pltpu.VMEM(grid.shape, jnp.bfloat16),
            pltpu.VMEM(factor.shape, jnp.bfloat16),
            pltpu.VMEM(local_inverse.shape, jnp.bfloat16),
            pltpu.VMEM((2, NOV, BLOCK, BLOCK), jnp.bfloat16),
            pltpu.VMEM((BLOCKS, 4, 2, BLOCK), jnp.bfloat16),
            pltpu.VMEM((64, 4, 16, 2, BLOCK), jnp.bfloat16),
            pltpu.VMEM((4, 2, BLOCKS, 2, BLOCK), jnp.bfloat16),
            pltpu.VMEM((4, 2, NOV), jnp.int32),
            pltpu.SMEM((4, 2, NOV), jnp.int32),
            pltpu.SMEM((4, 2, NOV), jnp.int32),
            pltpu.SMEM((4, 2, NOV), jnp.int32),
            pltpu.SMEM((2,), jnp.int32),
            dma, dma((4,)), dma((16,)), dma((16,)), dma((4,)), dma((4,)), dma((5,)),
            dma((2,)), dma((2,)), dma((8 * CHUNKS,)), dma((8 * CHUNKS,)),
            dma((SLOTS * CHUNKS,)), dma((SLOTS * CHUNKS,)),
        ],
        compiler_params=pltpu.CompilerParams(
            collective_id=0, has_side_effects=True, vmem_limit_bytes=28 * 2**20
        ),
        cost_estimate=pl.CostEstimate(
            flops=2 * 10**9, bytes_accessed=20 * 2**20, transcendentals=0
        ),
    )(*[
        pltpu.with_memory_space_constraint(value, pltpu.HBM)
        for value in (counts, grid, margin, factor, local_inverse)
    ])


def update_kernel(
    sub_ref, live_ref, flipped_ref, alive_ref, local_ref, ordered, diag_ref,
    stage, cross_out, cross_in, c_send, c_recv, k_send, k_recv,
):
    front = lax.axis_index("front")
    row = lax.axis_index("row")
    x, core = front // 2, front % 2
    z, y = row // 4, row % 4
    mine = (y * (1 - core) + z * core) % 2
    pair_up = partners(x, core, y, z, 1)
    pair_down = partners(x, core, y, z, 3)
    barrier = pltpu.get_barrier_semaphore()
    for other in (pair_up, pair_down):
        pl.semaphore_signal(barrier, inc=1, device_id=other, device_id_type=MESH)

    sends = []

    def block(a, b):
        return sub_ref[first_block(a) + b - a]

    def pair(index, cols):
        a = 2 * index
        direct = jnp.concatenate(
            [
                jnp.concatenate([block(a, b) for b in range(a, NOV)], axis=1),
                jnp.concatenate(
                    [block(a, a + 1).T] + [block(a + 1, b) for b in range(a + 1, NOV)], axis=1
                ),
            ],
            axis=0,
        )
        result = jnp.dot(direct, live_ref[a * BLOCK :, cols], preferred_element_type=jnp.float32)
        if index:
            mirrored = jnp.concatenate(
                [jnp.concatenate([block(b, a), block(b, a + 1)], axis=1) for b in range(a)], axis=0
            )
            turned = jnp.dot(
                flipped_ref[cols, : a * BLOCK], mirrored, preferred_element_type=jnp.float32
            )
            result = result + turned.T
        halves = []
        for half in range(2):
            value = -result[half * BLOCK : (half + 1) * BLOCK]
            value = jnp.where(alive_ref[a + half, :1, : cols.stop - cols.start] > 0, value, jnp.zeros_like(value))
            halves.append(value.astype(jnp.bfloat16))
        return halves

    def send(source, target, send_sem, recv_sem, device):
        copy = pltpu.make_async_remote_copy(
            src_ref=source, dst_ref=target, send_sem=send_sem, recv_sem=recv_sem,
            device_id=device, device_id_type=MESH,
        )
        copy.start()
        sends.append(copy)

    def returned(part, first, number):
        return ordered.at[part, pl.ds(first, 4), :, pl.ds(number * BLOCK, BLOCK)]

    def cross(cols, value):
        return jnp.dot(
            flipped_ref[cols, :], value.reshape(NOV * BLOCK, 256),
            preferred_element_type=jnp.float32,
        )

    own, lent, both = slice(0, 256), slice(256, 512), slice(0, 512)
    order_of_work = [(index, both) for index in range(4)]
    order_of_work += [(index, lent) for index in range(4, 8)]
    order_of_work += [(index, own) for index in range(4, 8)]
    for index, cols in order_of_work:
        halves = pair(index, cols)
        for half in range(2):
            at = 2 * index + half
            if cols is not lent:
                ordered[mine, at] = halves[half][:, :256]
            if cols is not own:
                stage[0, at] = halves[half][:, -256:-128]
                stage[1, at] = halves[half][:, -128:]
        if cols is own:
            continue
        if index == 1:
            pl.semaphore_wait(barrier, 2)
        if index % 2 == 2 - 1 and index:
            for done in (0, 1) if index == 1 and 2 == 1 else (index // 2,):
                for number, device in enumerate((pair_down, pair_up)):
                    slot = 2 * done + number
                    send(
                        stage.at[number, pl.ds(4 * done, 4)],
                        returned(mine, 4 * done, number),
                        c_send.at[slot], c_recv.at[slot], device,
                    )
        if index == 7:
            total = cross(lent, jnp.concatenate([stage[0], stage[1]], axis=2))
            for number, device in enumerate((pair_down, pair_up)):
                at = slice(number * BLOCK, (number + 1) * BLOCK)
                cross_out[number] = -total[at, at]
                send(
                    cross_out.at[number], cross_in.at[number],
                    k_send.at[number], k_recv.at[number], device,
                )
    total = cross(own, ordered[mine])

    for number in range(2):
        at = slice(number * BLOCK, (number + 1) * BLOCK)
        diag_ref[mine, number] = local_ref[mine, at, at] - total[at, at]
    for number in range(2):
        at = slice(number * BLOCK, (number + 1) * BLOCK)
        pltpu.make_async_copy(cross_in.at[number], cross_in.at[number], k_recv.at[number]).wait()
        diag_ref[1 - mine, number] = local_ref[1 - mine, at, at] + cross_in[number]
    for quarter in range(4):
        for number in range(2):
            ref = returned(1 - mine, quarter * 4, number)
            pltpu.make_async_copy(ref, ref, c_recv.at[2 * quarter + number]).wait()
    for copy in sends:
        copy.wait_send()


def restore_kernel(margin_ref, ordered_ref, diag_in, coupling_ref, diag_ref, sems):
    diag_copy = pltpu.make_async_copy(diag_in, diag_ref, sems.at[2])
    diag_copy.start()
    for part in range(2):
        keys = [order(margin_ref[part, a]) for a in range(NOV)]
        for a in range(NOV):
            at = sum((keys[b] < keys[a]).astype(jnp.int32) for b in range(NOV) if b != a)
            pltpu.make_async_copy(
                ordered_ref.at[part, at],
                coupling_ref.at[part, pl.ds(a * BLOCK, BLOCK)],
                sems.at[part],
            ).start()
    for part in range(2):
        whole = coupling_ref.at[part]
        pltpu.make_async_copy(whole, whole, sems.at[part]).wait()
    diag_copy.wait()


def body(parent, margin, counts, factor, local_inverse):
    sub, live, flipped, alive, local = gathered(parent, margin, counts, factor, local_inverse)
    vmem = pl.BlockSpec(memory_space=pltpu.VMEM)
    dma = pltpu.SemaphoreType.DMA
    ordered, diag = pl.pallas_call(
        update_kernel,
        out_shape=(
            jax.ShapeDtypeStruct((2, NOV, BLOCK, 256), jnp.bfloat16),
            jax.ShapeDtypeStruct((2, 2, BLOCK, BLOCK), jnp.float32),
        ),
        in_specs=[vmem] * 5,
        out_specs=(vmem, vmem),
        scratch_shapes=[
            pltpu.VMEM((2, NOV, BLOCK, BLOCK), jnp.bfloat16),
            pltpu.VMEM((2, BLOCK, BLOCK), jnp.float32),
            pltpu.VMEM((2, BLOCK, BLOCK), jnp.float32),
            dma((8,)), dma((8,)), dma((2,)), dma((2,)),
        ],
        compiler_params=pltpu.CompilerParams(
            collective_id=1, has_side_effects=True, vmem_limit_bytes=24 * 2**20
        ),
        cost_estimate=pl.CostEstimate(
            flops=6 * 10**9, bytes_accessed=20 * 2**20, transcendentals=0
        ),
    )(sub.reshape(BLOCKS, BLOCK, BLOCK), live, flipped, alive, local)
    hbm = pl.BlockSpec(memory_space=pl.ANY)
    return pl.pallas_call(
        restore_kernel,
        out_shape=(
            jax.ShapeDtypeStruct(factor.shape, jnp.bfloat16),
            jax.ShapeDtypeStruct((2, 2, BLOCK, BLOCK), jnp.float32),
        ),
        in_specs=[pl.BlockSpec(memory_space=pltpu.SMEM), vmem, vmem],
        out_specs=(hbm, hbm),
        scratch_shapes=[dma((3,))],
        compiler_params=pltpu.CompilerParams(vmem_limit_bytes=8 * 2**20),
    )(margin, ordered, diag)


def solution(mesh):
    placed = (
        P(("front", "row"), None),
        P("front", None),
        P("front"),
        P("front", None, "row"),
        P("front", None, "row"),
    )
    return jax.shard_map(
        body,
        mesh=mesh,
        in_specs=placed,
        out_specs=(P("front", None, "row"), P("front", "row", None, None)),
        check_vma=False,
    )
```

```python
import functools

import jax
import jax.numpy as jnp
from jax import lax
from jax.experimental import pallas as pl
from jax.experimental.pallas import tpu as pltpu
from jax.sharding import PartitionSpec as P

MESH = pl.DeviceIdType.MESH
NOV = 16
BLOCK = 128
BLOCKS = 136
CUTS = (0, 2, 6, 16)
CHUNKS = len(CUTS) - 1
SLOTS = 20


def place(x, core, y, z):
    return (2 * x + core, 4 * z + y)


def first_block(a):
    return NOV * a - a * (a - 1) // 2


def order(block):
    x, core, z, yh = block >> 4, (block >> 3) & 1, (block >> 1) & 3, block & 1
    group = z * (1 - core) + (7 - z) * core
    return group * 8 + x * 2 + yh


def network(count):
    swaps, p = [], 1
    while p < count:
        k = p
        while k >= 1:
            for j in range(k % p, count - k, 2 * k):
                for i in range(min(k, count - j - k)):
                    if (i + j) // (2 * p) == (i + j + k) // (2 * p):
                        swaps.append((i + j, i + j + k))
            k //= 2
        p *= 2
    return swaps


def columns(core, z):
    return (2 * z, 16 - 2 * z) if core == 0 else (8, 2 * z + 2)


def spans(chunk):
    first, last = first_block(CUTS[chunk]), first_block(CUTS[chunk + 1])
    return first, last - first


def partners(x, core, y, z, up):
    return place(x, core, (y + up * (1 - core)) % 4, (z + up * core) % 4)


def others(x, core, y, z, up):
    return place(x, core, (y + up * core) % 4, (z + up * (1 - core)) % 4)


def prepare_factor(
    count, part, ranked, factor_buf, lent_buf, live_ref, flipped_ref, alive_ref
):
    def mask(at, _):
        a = ranked(at)
        rows = pl.multiple_of(at * BLOCK, BLOCK)
        value = jnp.concatenate([factor_buf[part, a], lent_buf[0, a], lent_buf[1, a]], axis=1)
        value = jnp.where(a < count, value, jnp.zeros_like(value))
        live_ref[pl.ds(rows, BLOCK), :] = value
        flipped_ref[:, pl.ds(rows, BLOCK)] = value.T
        ones = jnp.ones((8, 512), jnp.float32)
        alive_ref[at] = jnp.where(a < count, ones, jnp.zeros_like(ones))
        return 0

    lax.fori_loop(0, NOV, mask, 0)


def prepare_local(part, first_col, inverse_buf, local_ref):
    def local(step, total):
        rows = pl.multiple_of(step * 512, 512)
        value = inverse_buf[part, pl.ds(rows, 512), :]
        row_at = rows + lax.broadcasted_iota(jnp.int32, value.shape, 0)
        col_at = first_col + lax.broadcasted_iota(jnp.int32, value.shape, 1)
        value = jnp.where(row_at >= col_at, value, jnp.zeros_like(value))
        return total + lax.dot_general(
            value, value, (((0,), (0,)), ((), ())), preferred_element_type=jnp.float32
        )

    local_ref[part] = lax.fori_loop(0, 8, local, jnp.zeros((256, 256), jnp.float32))


def gather_kernel(
    counts_ref, parent_ref, margin_ref, factor_ref, inverse_ref,
    out_ref, live_ref, flipped_ref, alive_ref, local_ref,
    parent_buf, factor_buf, inverse_buf, lent_buf, other_buf, slabs, picked, margin_buf, margin_smem, sorted_smem, ranked_smem, counts_smem,
    t_send, t_recv, d_send, d_recv, m_send, m_recv, l_sem, f_send, f_recv, x_send, x_recv, g_send, g_recv,
):
    front = lax.axis_index("front")
    row = lax.axis_index("row")
    x, core = front // 2, front % 2
    z, y = row // 4, row % 4
    half, yh = y % 2, y // 2
    fold = half * 2 + yh
    me_q = yh * 16 + z * 4 + x
    my_block = 16 * x + 8 * core + 2 * z + yh
    here = y * (1 - core) + z * core
    there = z * (1 - core) + y * core
    mine = here % 2
    sibling = place(x, 1 - core, y, z)
    pair_up = partners(x, core, y, z, 1)
    pair_down = partners(x, core, y, z, 3)
    pair_far = partners(x, core, y, z, 2)
    ring_up = others(x, core, y, z, 1)
    ring_down = others(x, core, y, z, 3)
    y_up = place(x, core, (y + 1) % 4, z)
    y_down = place(x, core, (y + 3) % 4, z)

    def member(q):
        return place(q % 4, core, 2 * (q // 16) + half, (q // 4) % 4)

    parent_load = pltpu.make_async_copy(parent_ref, parent_buf, l_sem.at[0])
    parent_load.start()
    factor_load = pltpu.make_async_copy(factor_ref, factor_buf, l_sem.at[1])
    factor_load.start()
    inverse_load = pltpu.make_async_copy(inverse_ref, inverse_buf, l_sem.at[2])
    inverse_load.start()
    counts_load = pltpu.make_async_copy(counts_ref, counts_smem, l_sem.at[4])
    counts_load.start()

    barrier = pltpu.get_barrier_semaphore()

    def greet(step, _):
        pl.semaphore_signal(
            barrier, inc=1, device_id=member((me_q + step) % 32), device_id_type=MESH
        )
        return 0

    lax.fori_loop(1, 32, greet, 0, unroll=True)
    for other in (sibling, y_up, y_down):
        pl.semaphore_signal(barrier, inc=1, device_id=other, device_id_type=MESH)
    parent_load.wait()
    pl.semaphore_wait(barrier, 34)

    margin_sends = []
    for step in (1, 2, 3):
        copy = pltpu.make_async_remote_copy(
            src_ref=margin_ref,
            dst_ref=margin_buf.at[x],
            send_sem=m_send.at[step],
            recv_sem=m_recv.at[x],
            device_id=place((x + step) % 4, core, y, z),
            device_id_type=MESH,
        )
        copy.start()
        margin_sends.append(copy)
    pltpu.make_async_copy(margin_ref, margin_buf.at[x], m_recv.at[x]).start()

    def spread_all(own_core, own_z):
        cols = pl.ds(*columns(own_core, own_z))
        pltpu.make_async_copy(
            parent_buf.at[me_q // 4, :, cols, me_q % 4],
            slabs.at[my_block, :, cols],
            t_recv.at[x],
        ).start()
        for offset in (0, 1, 3, 2):

            def spread(step, _):
                q = (yh * 4 + z + step) % 8 * 4 + (x + offset) % 4
                pltpu.make_async_remote_copy(
                    src_ref=parent_buf.at[q // 4, :, cols, q % 4],
                    dst_ref=slabs.at[my_block, :, cols],
                    send_sem=t_send,
                    recv_sem=t_recv.at[x],
                    device_id=member(q),
                    device_id_type=MESH,
                ).start()
                return 0

            lax.fori_loop(0 if offset else 1, 8, spread, 0)

    for own_core in range(2):
        for own_z in range(4):
            pl.when(jnp.logical_and(core == own_core, z == own_z))(
                functools.partial(spread_all, own_core, own_z)
            )

    factor_load.wait()
    lends = []
    for number, device in enumerate((pair_up, pair_down)):
        copy = pltpu.make_async_remote_copy(
            src_ref=factor_buf.at[1 - mine, :, :, pl.ds(number * BLOCK, BLOCK)],
            dst_ref=lent_buf.at[number],
            send_sem=f_send.at[number],
            recv_sem=f_recv.at[number],
            device_id=device,
            device_id_type=MESH,
        )
        copy.start()
        lends.append(copy)

    for source in range(4):
        pltpu.make_async_copy(margin_ref, margin_buf.at[source], m_recv.at[source]).wait()
    to_smem = pltpu.make_async_copy(margin_buf, margin_smem, l_sem.at[3])
    to_smem.start()
    to_smem.wait()

    swaps = network(NOV)

    def sort(index, _):
        target, part = index // 2, index % 2
        keys = []
        for a in range(NOV):
            block = margin_smem[target, part, a]
            keys.append(order(block) * 1024 + block * NOV + a)
        for i, j in swaps:
            keys[i], keys[j] = jnp.minimum(keys[i], keys[j]), jnp.maximum(keys[i], keys[j])
        for a in range(NOV):
            sorted_smem[target, part, a] = (keys[a] >> 4) & 63
            ranked_smem[target, part, a] = keys[a] & (NOV - 1)
        return 0

    lax.fori_loop(0, 8, sort, 0)

    def swap_cores(own_core, wait_only):
        total = sum(columns(own_core, own_z)[1] for own_z in range(4)) // 4
        for offset in (0, 1, 3, 2):
            source = (x + 4 - offset) % 4
            if not wait_only:
                group = slabs.at[pl.ds(0, 8), :, pl.ds(0, total)]
                pltpu.make_async_copy(group, group, t_recv.at[source]).wait()
            for own_z in range(4):
                part = slabs.at[
                    pl.ds(16 * source + 8 * own_core + 2 * own_z, 2), :,
                    pl.ds(*columns(own_core, own_z)),
                ]
                slot = 4 * source + own_z
                if wait_only:
                    pltpu.make_async_copy(part, part, d_recv.at[slot]).wait()
                else:
                    pltpu.make_async_remote_copy(
                        src_ref=part,
                        dst_ref=part,
                        send_sem=d_send.at[slot],
                        recv_sem=d_recv.at[slot],
                        device_id=sibling,
                        device_id_type=MESH,
                    ).start()

    def swap_sent(own_core):
        for source in range(4):
            for own_z in range(4):
                part = slabs.at[
                    pl.ds(16 * source + 8 * own_core + 2 * own_z, 2), :,
                    pl.ds(*columns(own_core, own_z)),
                ]
                pltpu.make_async_copy(part, part, d_send.at[4 * source + own_z]).wait()

    for own_core in range(2):
        pl.when(core == own_core)(functools.partial(swap_cores, own_core, False))

    for own_core in range(2):
        pl.when(core == 1 - own_core)(functools.partial(swap_cores, own_core, True))

    x_copies = [[] for _ in range(CHUNKS)]

    def start_x(chunk):
        blocks = pl.ds(*spans(chunk))
        for step in (2, 1, 3, 0):
            target = (x + step) % 4

            def pick(part, _):
                ids = [sorted_smem[target, part, a] for a in range(NOV)]
                for a in range(CUTS[chunk], CUTS[chunk + 1]):
                    for b in range(a, NOV):
                        block = slabs[ids[a], ids[b] >> 4, ids[b] & 15]
                        picked[target, part, first_block(a) + b - a] = block
                return 0

            lax.fori_loop(0, 2, pick, 0)
            slot = 8 * chunk + 2 * step
            lands = (out_ref.at[blocks, fold, z, x], other_buf.at[blocks, x])
            for number, land in enumerate(lands):
                part = (mine + number) % 2
                if step:
                    copy = pltpu.make_async_remote_copy(
                        src_ref=picked.at[target, part, blocks],
                        dst_ref=land,
                        send_sem=x_send.at[slot + number],
                        recv_sem=x_recv.at[slot + number],
                        device_id=place(target, core, y, z),
                        device_id_type=MESH,
                    )
                else:
                    copy = pltpu.make_async_copy(
                        picked.at[target, part, blocks], land, x_recv.at[slot + number]
                    )
                copy.start()
                x_copies[chunk].append(copy)

    sends = []

    def piece(chunk, pair_at, ring_at, side=None):
        y_at = pair_at * (1 - core) + ring_at * core
        z_at = ring_at * (1 - core) + pair_at * core
        first, count = spans(chunk)
        if side == 0:
            count = count // 2
        if side == 1:
            first, count = first + count // 2, count - count // 2
        return out_ref.at[pl.ds(first, count), (y_at % 2) * 2 + y_at // 2, z_at]

    def send(chunk, slot, source, target, device):
        at = SLOTS * chunk + slot
        copy = pltpu.make_async_remote_copy(
            src_ref=source, dst_ref=target, send_sem=g_send.at[at], recv_sem=g_recv.at[at],
            device_id=device, device_id_type=MESH,
        )
        copy.start()
        sends.append(copy)

    def landed(chunk, slot, ref):
        pltpu.make_async_copy(ref, ref, g_recv.at[SLOTS * chunk + slot]).wait()

    pair_places = (here, (here + 3) % 4, (here + 1) % 4, (here + 2) % 4)
    above, below, far = (there + 1) % 4, (there + 3) % 4, (there + 2) % 4

    def ring_direct(chunk, number):
        own = piece(chunk, pair_places[number], there)
        send(chunk, 4 + 4 * number, own, own, ring_up)
        send(chunk, 5 + 4 * number, own, own, ring_down)

    def ring_forward(chunk, number):
        at = pair_places[number]
        landed(chunk, 4 + 4 * number, piece(chunk, at, below))
        low = piece(chunk, at, below, 0)
        send(chunk, 6 + 4 * number, low, low, ring_up)
        landed(chunk, 5 + 4 * number, piece(chunk, at, above))
        high = piece(chunk, at, above, 1)
        send(chunk, 7 + 4 * number, high, high, ring_down)

    def step_own(chunk):
        for copy in x_copies[chunk]:
            copy.wait()
        own = piece(chunk, here, there)
        other = other_buf.at[pl.ds(*spans(chunk))]
        send(chunk, 0, other, own, pair_up)
        send(chunk, 1, other, own, pair_down)
        send(chunk, 2, own, own, pair_far)
        ring_direct(chunk, 0)

    def step_near(chunk):
        for number in (1, 2, 3):
            landed(chunk, number - 1, piece(chunk, pair_places[number], there))
            ring_direct(chunk, number)
        ring_forward(chunk, 0)

    def step_far(chunk):
        for number in (1, 2, 3):
            ring_forward(chunk, number)

    def step_end(chunk):
        for number, at in enumerate(pair_places):
            landed(chunk, 6 + 4 * number, piece(chunk, at, far, 0))
            landed(chunk, 7 + 4 * number, piece(chunk, at, far, 1))

    start_x(0)
    start_x(1)
    for turn in range(CHUNKS + 3):
        for delay, step in enumerate((step_own, step_near, step_far, step_end)):
            if 0 <= turn - delay < CHUNKS:
                step(turn - delay)
                if delay == 0 and turn + 2 < CHUNKS:
                    start_x(turn + 2)
        if turn == min(1, CHUNKS - 1):
            for copy in lends:
                copy.wait()
            counts_load.wait()
            prepare_factor(
                counts_smem[mine], mine, lambda at: ranked_smem[x, mine, at],
                factor_buf, lent_buf, live_ref, flipped_ref, alive_ref,
            )
        if turn == min(2, CHUNKS):
            inverse_load.wait()
            for part in range(2):
                prepare_local(part, row * 256, inverse_buf, local_ref)

    for copy in sends:
        copy.wait_send()
    for copy in margin_sends:
        copy.wait_send()

    def spread_sent(own_core, own_z):
        sent = slabs.at[pl.ds(0, 31), :, pl.ds(0, columns(own_core, own_z)[1])]
        pltpu.make_async_copy(sent, sent, t_send).wait()

    for own_core in range(2):
        pl.when(core == own_core)(functools.partial(swap_sent, own_core))
        for own_z in range(4):
            pl.when(jnp.logical_and(core == own_core, z == own_z))(
                functools.partial(spread_sent, own_core, own_z)
            )


def gathered(parent, margin, counts, factor, local_inverse):
    grid = parent.reshape(8, 4, 2, 4, 16, BLOCK).transpose(0, 3, 4, 1, 2, 5)
    factor = factor.reshape(2, NOV, BLOCK, 256)
    dma = pltpu.SemaphoreType.DMA
    vmem = pl.BlockSpec(memory_space=pltpu.VMEM)
    hbm = pl.BlockSpec(memory_space=pltpu.HBM)
    return pl.pallas_call(
        gather_kernel,
        out_shape=(
            jax.ShapeDtypeStruct((BLOCKS, 4, 4, 4, 2, BLOCK), jnp.bfloat16),
            jax.ShapeDtypeStruct((2048, 512), jnp.bfloat16),
            jax.ShapeDtypeStruct((512, 2048), jnp.bfloat16),
            jax.ShapeDtypeStruct((NOV, 8, 512), jnp.float32),
            jax.ShapeDtypeStruct((2, 256, 256), jnp.float32),
        ),
        in_specs=[hbm] * 5,
        out_specs=(vmem,) * 5,
        scratch_shapes=[
            pltpu.VMEM(grid.shape, jnp.bfloat16),
            pltpu.VMEM(factor.shape, jnp.bfloat16),
            pltpu.VMEM(local_inverse.shape, jnp.bfloat16),
            pltpu.VMEM((2, NOV, BLOCK, BLOCK), jnp.bfloat16),
            pltpu.VMEM((BLOCKS, 4, 2, BLOCK), jnp.bfloat16),
            pltpu.VMEM((64, 4, 16, 2, BLOCK), jnp.bfloat16),
            pltpu.VMEM((4, 2, BLOCKS, 2, BLOCK), jnp.bfloat16),
            pltpu.VMEM((4, 2, NOV), jnp.int32),
            pltpu.SMEM((4, 2, NOV), jnp.int32),
            pltpu.SMEM((4, 2, NOV), jnp.int32),
            pltpu.SMEM((4, 2, NOV), jnp.int32),
            pltpu.SMEM((2,), jnp.int32),
            dma, dma((4,)), dma((16,)), dma((16,)), dma((4,)), dma((4,)), dma((5,)),
            dma((2,)), dma((2,)), dma((8 * CHUNKS,)), dma((8 * CHUNKS,)),
            dma((SLOTS * CHUNKS,)), dma((SLOTS * CHUNKS,)),
        ],
        compiler_params=pltpu.CompilerParams(
            collective_id=0, has_side_effects=True, vmem_limit_bytes=28 * 2**20
        ),
        cost_estimate=pl.CostEstimate(
            flops=2 * 10**9, bytes_accessed=20 * 2**20, transcendentals=0
        ),
    )(*[
        pltpu.with_memory_space_constraint(value, pltpu.HBM)
        for value in (counts, grid, margin, factor, local_inverse)
    ])


def update_kernel(
    sub_ref, live_ref, flipped_ref, alive_ref, local_ref, ordered, diag_ref,
    stage, cross_out, cross_in, c_send, c_recv, k_send, k_recv,
):
    front = lax.axis_index("front")
    row = lax.axis_index("row")
    x, core = front // 2, front % 2
    z, y = row // 4, row % 4
    mine = (y * (1 - core) + z * core) % 2
    pair_up = partners(x, core, y, z, 1)
    pair_down = partners(x, core, y, z, 3)
    barrier = pltpu.get_barrier_semaphore()
    for other in (pair_up, pair_down):
        pl.semaphore_signal(barrier, inc=1, device_id=other, device_id_type=MESH)

    sends = []

    def block(a, b):
        return sub_ref[first_block(a) + b - a]

    def pair(index, cols):
        a = 2 * index
        direct = jnp.concatenate(
            [
                jnp.concatenate([block(a, b) for b in range(a, NOV)], axis=1),
                jnp.concatenate(
                    [block(a, a + 1).T] + [block(a + 1, b) for b in range(a + 1, NOV)], axis=1
                ),
            ],
            axis=0,
        )
        result = jnp.dot(direct, live_ref[a * BLOCK :, cols], preferred_element_type=jnp.float32)
        if index:
            mirrored = jnp.concatenate(
                [jnp.concatenate([block(b, a), block(b, a + 1)], axis=1) for b in range(a)], axis=0
            )
            turned = jnp.dot(
                flipped_ref[cols, : a * BLOCK], mirrored, preferred_element_type=jnp.float32
            )
            result = result + turned.T
        halves = []
        for half in range(2):
            value = -result[half * BLOCK : (half + 1) * BLOCK]
            value = jnp.where(alive_ref[a + half, :1, : cols.stop - cols.start] > 0, value, jnp.zeros_like(value))
            halves.append(value.astype(jnp.bfloat16))
        return halves

    def send(source, target, send_sem, recv_sem, device):
        copy = pltpu.make_async_remote_copy(
            src_ref=source, dst_ref=target, send_sem=send_sem, recv_sem=recv_sem,
            device_id=device, device_id_type=MESH,
        )
        copy.start()
        sends.append(copy)

    def returned(part, first, number):
        return ordered.at[part, pl.ds(first, 4), :, pl.ds(number * BLOCK, BLOCK)]

    def cross(cols, value):
        return jnp.dot(
            flipped_ref[cols, :], value.reshape(NOV * BLOCK, 256),
            preferred_element_type=jnp.float32,
        )

    own, lent, both = slice(0, 256), slice(256, 512), slice(0, 512)
    order_of_work = [(index, both) for index in range(5)]
    order_of_work += [(index, lent) for index in range(5, 8)]
    order_of_work += [(index, own) for index in range(5, 8)]
    for index, cols in order_of_work:
        halves = pair(index, cols)
        for half in range(2):
            at = 2 * index + half
            if cols is not lent:
                ordered[mine, at] = halves[half][:, :256]
            if cols is not own:
                stage[0, at] = halves[half][:, -256:-128]
                stage[1, at] = halves[half][:, -128:]
        if cols is own:
            continue
        if index == 1:
            pl.semaphore_wait(barrier, 2)
        if index % 2 == 2 - 1 and index:
            for done in (0, 1) if index == 1 and 2 == 1 else (index // 2,):
                for number, device in enumerate((pair_down, pair_up)):
                    slot = 2 * done + number
                    send(
                        stage.at[number, pl.ds(4 * done, 4)],
                        returned(mine, 4 * done, number),
                        c_send.at[slot], c_recv.at[slot], device,
                    )
        if index == 7:
            total = cross(lent, jnp.concatenate([stage[0], stage[1]], axis=2))
            for number, device in enumerate((pair_down, pair_up)):
                at = slice(number * BLOCK, (number + 1) * BLOCK)
                cross_out[number] = -total[at, at]
                send(
                    cross_out.at[number], cross_in.at[number],
                    k_send.at[number], k_recv.at[number], device,
                )
    total = cross(own, ordered[mine])

    for number in range(2):
        at = slice(number * BLOCK, (number + 1) * BLOCK)
        diag_ref[mine, number] = local_ref[mine, at, at] - total[at, at]
    for number in range(2):
        at = slice(number * BLOCK, (number + 1) * BLOCK)
        pltpu.make_async_copy(cross_in.at[number], cross_in.at[number], k_recv.at[number]).wait()
        diag_ref[1 - mine, number] = local_ref[1 - mine, at, at] + cross_in[number]
    for quarter in range(4):
        for number in range(2):
            ref = returned(1 - mine, quarter * 4, number)
            pltpu.make_async_copy(ref, ref, c_recv.at[2 * quarter + number]).wait()
    for copy in sends:
        copy.wait_send()


def restore_kernel(margin_ref, ordered_ref, diag_in, coupling_ref, diag_ref, sems):
    diag_copy = pltpu.make_async_copy(diag_in, diag_ref, sems.at[2])
    diag_copy.start()
    for part in range(2):
        keys = [order(margin_ref[part, a]) for a in range(NOV)]
        for a in range(NOV):
            at = sum((keys[b] < keys[a]).astype(jnp.int32) for b in range(NOV) if b != a)
            pltpu.make_async_copy(
                ordered_ref.at[part, at],
                coupling_ref.at[part, pl.ds(a * BLOCK, BLOCK)],
                sems.at[part],
            ).start()
    for part in range(2):
        whole = coupling_ref.at[part]
        pltpu.make_async_copy(whole, whole, sems.at[part]).wait()
    diag_copy.wait()


def body(parent, margin, counts, factor, local_inverse):
    sub, live, flipped, alive, local = gathered(parent, margin, counts, factor, local_inverse)
    vmem = pl.BlockSpec(memory_space=pltpu.VMEM)
    dma = pltpu.SemaphoreType.DMA
    ordered, diag = pl.pallas_call(
        update_kernel,
        out_shape=(
            jax.ShapeDtypeStruct((2, NOV, BLOCK, 256), jnp.bfloat16),
            jax.ShapeDtypeStruct((2, 2, BLOCK, BLOCK), jnp.float32),
        ),
        in_specs=[vmem] * 5,
        out_specs=(vmem, vmem),
        scratch_shapes=[
            pltpu.VMEM((2, NOV, BLOCK, BLOCK), jnp.bfloat16),
            pltpu.VMEM((2, BLOCK, BLOCK), jnp.float32),
            pltpu.VMEM((2, BLOCK, BLOCK), jnp.float32),
            dma((8,)), dma((8,)), dma((2,)), dma((2,)),
        ],
        compiler_params=pltpu.CompilerParams(
            collective_id=1, has_side_effects=True, vmem_limit_bytes=24 * 2**20
        ),
        cost_estimate=pl.CostEstimate(
            flops=6 * 10**9, bytes_accessed=20 * 2**20, transcendentals=0
        ),
    )(sub.reshape(BLOCKS, BLOCK, BLOCK), live, flipped, alive, local)
    hbm = pl.BlockSpec(memory_space=pl.ANY)
    return pl.pallas_call(
        restore_kernel,
        out_shape=(
            jax.ShapeDtypeStruct(factor.shape, jnp.bfloat16),
            jax.ShapeDtypeStruct((2, 2, BLOCK, BLOCK), jnp.float32),
        ),
        in_specs=[pl.BlockSpec(memory_space=pltpu.SMEM), vmem, vmem],
        out_specs=(hbm, hbm),
        scratch_shapes=[dma((3,))],
        compiler_params=pltpu.CompilerParams(vmem_limit_bytes=8 * 2**20),
    )(margin, ordered, diag)


def solution(mesh):
    placed = (
        P(("front", "row"), None),
        P("front", None),
        P("front"),
        P("front", None, "row"),
        P("front", None, "row"),
    )
    return jax.shard_map(
        body,
        mesh=mesh,
        in_specs=placed,
        out_specs=(P("front", None, "row"), P("front", "row", None, None)),
        check_vma=False,
    )
```

```python
import functools

import jax
import jax.numpy as jnp
from jax import lax
from jax.experimental import pallas as pl
from jax.experimental.pallas import tpu as pltpu
from jax.sharding import PartitionSpec as P

MESH = pl.DeviceIdType.MESH
NOV = 16
BLOCK = 128
BLOCKS = 136
CUTS = (0, 2, 6, 16)
CHUNKS = len(CUTS) - 1
SLOTS = 20


def place(x, core, y, z):
    return (2 * x + core, 4 * z + y)


def first_block(a):
    return NOV * a - a * (a - 1) // 2


def order(block):
    x, core, z, yh = block >> 4, (block >> 3) & 1, (block >> 1) & 3, block & 1
    group = z * (1 - core) + (7 - z) * core
    return group * 8 + x * 2 + yh


def network(count):
    swaps, p = [], 1
    while p < count:
        k = p
        while k >= 1:
            for j in range(k % p, count - k, 2 * k):
                for i in range(min(k, count - j - k)):
                    if (i + j) // (2 * p) == (i + j + k) // (2 * p):
                        swaps.append((i + j, i + j + k))
            k //= 2
        p *= 2
    return swaps


def columns(core, z):
    return (2 * z, 16 - 2 * z) if core == 0 else (8, 2 * z + 2)


def spans(chunk):
    first, last = first_block(CUTS[chunk]), first_block(CUTS[chunk + 1])
    return first, last - first


def partners(x, core, y, z, up):
    return place(x, core, (y + up * (1 - core)) % 4, (z + up * core) % 4)


def others(x, core, y, z, up):
    return place(x, core, (y + up * core) % 4, (z + up * (1 - core)) % 4)


def prepare_factor(
    count, part, ranked, factor_buf, lent_buf, live_ref, flipped_ref, alive_ref
):
    def mask(at, _):
        a = ranked(at)
        rows = pl.multiple_of(at * BLOCK, BLOCK)
        value = jnp.concatenate([factor_buf[part, a], lent_buf[0, a], lent_buf[1, a]], axis=1)
        value = jnp.where(a < count, value, jnp.zeros_like(value))
        live_ref[pl.ds(rows, BLOCK), :] = value
        flipped_ref[:, pl.ds(rows, BLOCK)] = value.T
        ones = jnp.ones((8, 512), jnp.float32)
        alive_ref[at] = jnp.where(a < count, ones, jnp.zeros_like(ones))
        return 0

    lax.fori_loop(0, NOV, mask, 0)


def prepare_local(part, first_col, inverse_buf, local_ref):
    def local(step, total):
        rows = pl.multiple_of(step * 512, 512)
        value = inverse_buf[part, pl.ds(rows, 512), :]
        row_at = rows + lax.broadcasted_iota(jnp.int32, value.shape, 0)
        col_at = first_col + lax.broadcasted_iota(jnp.int32, value.shape, 1)
        value = jnp.where(row_at >= col_at, value, jnp.zeros_like(value))
        return total + lax.dot_general(
            value, value, (((0,), (0,)), ((), ())), preferred_element_type=jnp.float32
        )

    local_ref[part] = lax.fori_loop(0, 8, local, jnp.zeros((256, 256), jnp.float32))


def gather_kernel(
    counts_ref, parent_ref, margin_ref, factor_ref, inverse_ref,
    out_ref, live_ref, flipped_ref, alive_ref, local_ref,
    parent_buf, factor_buf, inverse_buf, lent_buf, other_buf, slabs, picked, margin_buf, margin_smem, sorted_smem, ranked_smem, counts_smem,
    t_send, t_recv, d_send, d_recv, m_send, m_recv, l_sem, f_send, f_recv, x_send, x_recv, g_send, g_recv,
):
    front = lax.axis_index("front")
    row = lax.axis_index("row")
    x, core = front // 2, front % 2
    z, y = row // 4, row % 4
    half, yh = y % 2, y // 2
    fold = half * 2 + yh
    me_q = yh * 16 + z * 4 + x
    my_block = 16 * x + 8 * core + 2 * z + yh
    here = y * (1 - core) + z * core
    there = z * (1 - core) + y * core
    mine = here % 2
    sibling = place(x, 1 - core, y, z)
    pair_up = partners(x, core, y, z, 1)
    pair_down = partners(x, core, y, z, 3)
    pair_far = partners(x, core, y, z, 2)
    ring_up = others(x, core, y, z, 1)
    ring_down = others(x, core, y, z, 3)
    y_up = place(x, core, (y + 1) % 4, z)
    y_down = place(x, core, (y + 3) % 4, z)

    def member(q):
        return place(q % 4, core, 2 * (q // 16) + half, (q // 4) % 4)

    parent_load = pltpu.make_async_copy(parent_ref, parent_buf, l_sem.at[0])
    parent_load.start()
    factor_load = pltpu.make_async_copy(factor_ref, factor_buf, l_sem.at[1])
    factor_load.start()
    inverse_load = pltpu.make_async_copy(inverse_ref, inverse_buf, l_sem.at[2])
    inverse_load.start()
    counts_load = pltpu.make_async_copy(counts_ref, counts_smem, l_sem.at[4])
    counts_load.start()

    barrier = pltpu.get_barrier_semaphore()

    def greet(step, _):
        pl.semaphore_signal(
            barrier, inc=1, device_id=member((me_q + step) % 32), device_id_type=MESH
        )
        return 0

    lax.fori_loop(1, 32, greet, 0, unroll=True)
    for other in (sibling, y_up, y_down):
        pl.semaphore_signal(barrier, inc=1, device_id=other, device_id_type=MESH)
    parent_load.wait()
    pl.semaphore_wait(barrier, 34)

    margin_sends = []
    for step in (1, 2, 3):
        copy = pltpu.make_async_remote_copy(
            src_ref=margin_ref,
            dst_ref=margin_buf.at[x],
            send_sem=m_send.at[step],
            recv_sem=m_recv.at[x],
            device_id=place((x + step) % 4, core, y, z),
            device_id_type=MESH,
        )
        copy.start()
        margin_sends.append(copy)
    pltpu.make_async_copy(margin_ref, margin_buf.at[x], m_recv.at[x]).start()

    def spread_all(own_core, own_z):
        cols = pl.ds(*columns(own_core, own_z))
        pltpu.make_async_copy(
            parent_buf.at[me_q // 4, :, cols, me_q % 4],
            slabs.at[my_block, :, cols],
            t_recv.at[x],
        ).start()
        for offset in (0, 1, 3, 2):

            def spread(step, _):
                q = (yh * 4 + z + step) % 8 * 4 + (x + offset) % 4
                pltpu.make_async_remote_copy(
                    src_ref=parent_buf.at[q // 4, :, cols, q % 4],
                    dst_ref=slabs.at[my_block, :, cols],
                    send_sem=t_send,
                    recv_sem=t_recv.at[x],
                    device_id=member(q),
                    device_id_type=MESH,
                ).start()
                return 0

            lax.fori_loop(0 if offset else 1, 8, spread, 0, unroll=True)

    for own_core in range(2):
        for own_z in range(4):
            pl.when(jnp.logical_and(core == own_core, z == own_z))(
                functools.partial(spread_all, own_core, own_z)
            )

    factor_load.wait()
    lends = []
    for number, device in enumerate((pair_up, pair_down)):
        copy = pltpu.make_async_remote_copy(
            src_ref=factor_buf.at[1 - mine, :, :, pl.ds(number * BLOCK, BLOCK)],
            dst_ref=lent_buf.at[number],
            send_sem=f_send.at[number],
            recv_sem=f_recv.at[number],
            device_id=device,
            device_id_type=MESH,
        )
        copy.start()
        lends.append(copy)

    for source in range(4):
        pltpu.make_async_copy(margin_ref, margin_buf.at[source], m_recv.at[source]).wait()
    to_smem = pltpu.make_async_copy(margin_buf, margin_smem, l_sem.at[3])
    to_smem.start()
    to_smem.wait()

    swaps = network(NOV)

    def sort(index, _):
        target, part = index // 2, index % 2
        keys = []
        for a in range(NOV):
            block = margin_smem[target, part, a]
            keys.append(order(block) * 1024 + block * NOV + a)
        for i, j in swaps:
            keys[i], keys[j] = jnp.minimum(keys[i], keys[j]), jnp.maximum(keys[i], keys[j])
        for a in range(NOV):
            sorted_smem[target, part, a] = (keys[a] >> 4) & 63
            ranked_smem[target, part, a] = keys[a] & (NOV - 1)
        return 0

    lax.fori_loop(0, 8, sort, 0)

    def swap_cores(own_core, wait_only):
        total = sum(columns(own_core, own_z)[1] for own_z in range(4)) // 4
        for offset in (0, 1, 3, 2):
            source = (x + 4 - offset) % 4
            if not wait_only:
                group = slabs.at[pl.ds(0, 8), :, pl.ds(0, total)]
                pltpu.make_async_copy(group, group, t_recv.at[source]).wait()
            for own_z in range(4):
                part = slabs.at[
                    pl.ds(16 * source + 8 * own_core + 2 * own_z, 2), :,
                    pl.ds(*columns(own_core, own_z)),
                ]
                slot = 4 * source + own_z
                if wait_only:
                    pltpu.make_async_copy(part, part, d_recv.at[slot]).wait()
                else:
                    pltpu.make_async_remote_copy(
                        src_ref=part,
                        dst_ref=part,
                        send_sem=d_send.at[slot],
                        recv_sem=d_recv.at[slot],
                        device_id=sibling,
                        device_id_type=MESH,
                    ).start()

    def swap_sent(own_core):
        for source in range(4):
            for own_z in range(4):
                part = slabs.at[
                    pl.ds(16 * source + 8 * own_core + 2 * own_z, 2), :,
                    pl.ds(*columns(own_core, own_z)),
                ]
                pltpu.make_async_copy(part, part, d_send.at[4 * source + own_z]).wait()

    for own_core in range(2):
        pl.when(core == own_core)(functools.partial(swap_cores, own_core, False))

    for own_core in range(2):
        pl.when(core == 1 - own_core)(functools.partial(swap_cores, own_core, True))

    x_copies = [[] for _ in range(CHUNKS)]

    def start_x(chunk):
        blocks = pl.ds(*spans(chunk))
        for step in (2, 1, 3, 0):
            target = (x + step) % 4

            def pick(part, _):
                ids = [sorted_smem[target, part, a] for a in range(NOV)]
                for a in range(CUTS[chunk], CUTS[chunk + 1]):
                    for b in range(a, NOV):
                        block = slabs[ids[a], ids[b] >> 4, ids[b] & 15]
                        picked[target, part, first_block(a) + b - a] = block
                return 0

            lax.fori_loop(0, 2, pick, 0)
            slot = 8 * chunk + 2 * step
            lands = (out_ref.at[blocks, fold, z, x], other_buf.at[blocks, x])
            for number, land in enumerate(lands):
                part = (mine + number) % 2
                if step:
                    copy = pltpu.make_async_remote_copy(
                        src_ref=picked.at[target, part, blocks],
                        dst_ref=land,
                        send_sem=x_send.at[slot + number],
                        recv_sem=x_recv.at[slot + number],
                        device_id=place(target, core, y, z),
                        device_id_type=MESH,
                    )
                else:
                    copy = pltpu.make_async_copy(
                        picked.at[target, part, blocks], land, x_recv.at[slot + number]
                    )
                copy.start()
                x_copies[chunk].append(copy)

    sends = []

    def piece(chunk, pair_at, ring_at, side=None):
        y_at = pair_at * (1 - core) + ring_at * core
        z_at = ring_at * (1 - core) + pair_at * core
        first, count = spans(chunk)
        if side == 0:
            count = count // 2
        if side == 1:
            first, count = first + count // 2, count - count // 2
        return out_ref.at[pl.ds(first, count), (y_at % 2) * 2 + y_at // 2, z_at]

    def send(chunk, slot, source, target, device):
        at = SLOTS * chunk + slot
        copy = pltpu.make_async_remote_copy(
            src_ref=source, dst_ref=target, send_sem=g_send.at[at], recv_sem=g_recv.at[at],
            device_id=device, device_id_type=MESH,
        )
        copy.start()
        sends.append(copy)

    def landed(chunk, slot, ref):
        pltpu.make_async_copy(ref, ref, g_recv.at[SLOTS * chunk + slot]).wait()

    pair_places = (here, (here + 3) % 4, (here + 1) % 4, (here + 2) % 4)
    above, below, far = (there + 1) % 4, (there + 3) % 4, (there + 2) % 4

    def ring_direct(chunk, number):
        own = piece(chunk, pair_places[number], there)
        send(chunk, 4 + 4 * number, own, own, ring_up)
        send(chunk, 5 + 4 * number, own, own, ring_down)

    def ring_forward(chunk, number):
        at = pair_places[number]
        landed(chunk, 4 + 4 * number, piece(chunk, at, below))
        low = piece(chunk, at, below, 0)
        send(chunk, 6 + 4 * number, low, low, ring_up)
        landed(chunk, 5 + 4 * number, piece(chunk, at, above))
        high = piece(chunk, at, above, 1)
        send(chunk, 7 + 4 * number, high, high, ring_down)

    def step_own(chunk):
        for copy in x_copies[chunk]:
            copy.wait()
        own = piece(chunk, here, there)
        other = other_buf.at[pl.ds(*spans(chunk))]
        send(chunk, 0, other, own, pair_up)
        send(chunk, 1, other, own, pair_down)
        send(chunk, 2, own, own, pair_far)
        ring_direct(chunk, 0)

    def step_near(chunk):
        for number in (1, 2, 3):
            landed(chunk, number - 1, piece(chunk, pair_places[number], there))
            ring_direct(chunk, number)
        ring_forward(chunk, 0)

    def step_far(chunk):
        for number in (1, 2, 3):
            ring_forward(chunk, number)

    def step_end(chunk):
        for number, at in enumerate(pair_places):
            landed(chunk, 6 + 4 * number, piece(chunk, at, far, 0))
            landed(chunk, 7 + 4 * number, piece(chunk, at, far, 1))

    start_x(0)
    start_x(1)
    for turn in range(CHUNKS + 3):
        for delay, step in enumerate((step_own, step_near, step_far, step_end)):
            if 0 <= turn - delay < CHUNKS:
                step(turn - delay)
                if delay == 0 and turn + 2 < CHUNKS:
                    start_x(turn + 2)
        if turn == min(1, CHUNKS - 1):
            for copy in lends:
                copy.wait()
            counts_load.wait()
            prepare_factor(
                counts_smem[mine], mine, lambda at: ranked_smem[x, mine, at],
                factor_buf, lent_buf, live_ref, flipped_ref, alive_ref,
            )
        if turn == min(2, CHUNKS):
            inverse_load.wait()
            for part in range(2):
                prepare_local(part, row * 256, inverse_buf, local_ref)

    for copy in sends:
        copy.wait_send()
    for copy in margin_sends:
        copy.wait_send()

    def spread_sent(own_core, own_z):
        sent = slabs.at[pl.ds(0, 31), :, pl.ds(0, columns(own_core, own_z)[1])]
        pltpu.make_async_copy(sent, sent, t_send).wait()

    for own_core in range(2):
        pl.when(core == own_core)(functools.partial(swap_sent, own_core))
        for own_z in range(4):
            pl.when(jnp.logical_and(core == own_core, z == own_z))(
                functools.partial(spread_sent, own_core, own_z)
            )


def gathered(parent, margin, counts, factor, local_inverse):
    grid = parent.reshape(8, 4, 2, 4, 16, BLOCK).transpose(0, 3, 4, 1, 2, 5)
    factor = factor.reshape(2, NOV, BLOCK, 256)
    dma = pltpu.SemaphoreType.DMA
    vmem = pl.BlockSpec(memory_space=pltpu.VMEM)
    hbm = pl.BlockSpec(memory_space=pltpu.HBM)
    return pl.pallas_call(
        gather_kernel,
        out_shape=(
            jax.ShapeDtypeStruct((BLOCKS, 4, 4, 4, 2, BLOCK), jnp.bfloat16),
            jax.ShapeDtypeStruct((2048, 512), jnp.bfloat16),
            jax.ShapeDtypeStruct((512, 2048), jnp.bfloat16),
            jax.ShapeDtypeStruct((NOV, 8, 512), jnp.float32),
            jax.ShapeDtypeStruct((2, 256, 256), jnp.float32),
        ),
        in_specs=[hbm] * 5,
        out_specs=(vmem,) * 5,
        scratch_shapes=[
            pltpu.VMEM(grid.shape, jnp.bfloat16),
            pltpu.VMEM(factor.shape, jnp.bfloat16),
            pltpu.VMEM(local_inverse.shape, jnp.bfloat16),
            pltpu.VMEM((2, NOV, BLOCK, BLOCK), jnp.bfloat16),
            pltpu.VMEM((BLOCKS, 4, 2, BLOCK), jnp.bfloat16),
            pltpu.VMEM((64, 4, 16, 2, BLOCK), jnp.bfloat16),
            pltpu.VMEM((4, 2, BLOCKS, 2, BLOCK), jnp.bfloat16),
            pltpu.VMEM((4, 2, NOV), jnp.int32),
            pltpu.SMEM((4, 2, NOV), jnp.int32),
            pltpu.SMEM((4, 2, NOV), jnp.int32),
            pltpu.SMEM((4, 2, NOV), jnp.int32),
            pltpu.SMEM((2,), jnp.int32),
            dma, dma((4,)), dma((16,)), dma((16,)), dma((4,)), dma((4,)), dma((5,)),
            dma((2,)), dma((2,)), dma((8 * CHUNKS,)), dma((8 * CHUNKS,)),
            dma((SLOTS * CHUNKS,)), dma((SLOTS * CHUNKS,)),
        ],
        compiler_params=pltpu.CompilerParams(
            collective_id=0, has_side_effects=True, vmem_limit_bytes=28 * 2**20
        ),
        cost_estimate=pl.CostEstimate(
            flops=2 * 10**9, bytes_accessed=20 * 2**20, transcendentals=0
        ),
    )(*[
        pltpu.with_memory_space_constraint(value, pltpu.HBM)
        for value in (counts, grid, margin, factor, local_inverse)
    ])


def update_kernel(
    sub_ref, live_ref, flipped_ref, alive_ref, local_ref, ordered, diag_ref,
    stage, cross_out, cross_in, c_send, c_recv, k_send, k_recv,
):
    front = lax.axis_index("front")
    row = lax.axis_index("row")
    x, core = front // 2, front % 2
    z, y = row // 4, row % 4
    mine = (y * (1 - core) + z * core) % 2
    pair_up = partners(x, core, y, z, 1)
    pair_down = partners(x, core, y, z, 3)
    barrier = pltpu.get_barrier_semaphore()
    for other in (pair_up, pair_down):
        pl.semaphore_signal(barrier, inc=1, device_id=other, device_id_type=MESH)

    sends = []

    def block(a, b):
        return sub_ref[first_block(a) + b - a]

    def pair(index, cols):
        a = 2 * index
        direct = jnp.concatenate(
            [
                jnp.concatenate([block(a, b) for b in range(a, NOV)], axis=1),
                jnp.concatenate(
                    [block(a, a + 1).T] + [block(a + 1, b) for b in range(a + 1, NOV)], axis=1
                ),
            ],
            axis=0,
        )
        result = jnp.dot(direct, live_ref[a * BLOCK :, cols], preferred_element_type=jnp.float32)
        if index:
            mirrored = jnp.concatenate(
                [jnp.concatenate([block(b, a), block(b, a + 1)], axis=1) for b in range(a)], axis=0
            )
            turned = jnp.dot(
                flipped_ref[cols, : a * BLOCK], mirrored, preferred_element_type=jnp.float32
            )
            result = result + turned.T
        halves = []
        for half in range(2):
            value = -result[half * BLOCK : (half + 1) * BLOCK]
            value = jnp.where(alive_ref[a + half, :1, : cols.stop - cols.start] > 0, value, jnp.zeros_like(value))
            halves.append(value.astype(jnp.bfloat16))
        return halves

    def send(source, target, send_sem, recv_sem, device):
        copy = pltpu.make_async_remote_copy(
            src_ref=source, dst_ref=target, send_sem=send_sem, recv_sem=recv_sem,
            device_id=device, device_id_type=MESH,
        )
        copy.start()
        sends.append(copy)

    def returned(part, first, number):
        return ordered.at[part, pl.ds(first, 4), :, pl.ds(number * BLOCK, BLOCK)]

    def cross(cols, value):
        return jnp.dot(
            flipped_ref[cols, :], value.reshape(NOV * BLOCK, 256),
            preferred_element_type=jnp.float32,
        )

    own, lent, both = slice(0, 256), slice(256, 512), slice(0, 512)
    order_of_work = [(index, both) for index in range(5)]
    order_of_work += [(index, lent) for index in range(5, 8)]
    order_of_work += [(index, own) for index in range(5, 8)]
    for index, cols in order_of_work:
        halves = pair(index, cols)
        for half in range(2):
            at = 2 * index + half
            if cols is not lent:
                ordered[mine, at] = halves[half][:, :256]
            if cols is not own:
                stage[0, at] = halves[half][:, -256:-128]
                stage[1, at] = halves[half][:, -128:]
        if cols is own:
            continue
        if index == 1:
            pl.semaphore_wait(barrier, 2)
        if index % 2 == 2 - 1 and index:
            for done in (0, 1) if index == 1 and 2 == 1 else (index // 2,):
                for number, device in enumerate((pair_down, pair_up)):
                    slot = 2 * done + number
                    send(
                        stage.at[number, pl.ds(4 * done, 4)],
                        returned(mine, 4 * done, number),
                        c_send.at[slot], c_recv.at[slot], device,
                    )
        if index == 7:
            total = cross(lent, jnp.concatenate([stage[0], stage[1]], axis=2))
            for number, device in enumerate((pair_down, pair_up)):
                at = slice(number * BLOCK, (number + 1) * BLOCK)
                cross_out[number] = -total[at, at]
                send(
                    cross_out.at[number], cross_in.at[number],
                    k_send.at[number], k_recv.at[number], device,
                )
    total = cross(own, ordered[mine])

    for number in range(2):
        at = slice(number * BLOCK, (number + 1) * BLOCK)
        diag_ref[mine, number] = local_ref[mine, at, at] - total[at, at]
    for number in range(2):
        at = slice(number * BLOCK, (number + 1) * BLOCK)
        pltpu.make_async_copy(cross_in.at[number], cross_in.at[number], k_recv.at[number]).wait()
        diag_ref[1 - mine, number] = local_ref[1 - mine, at, at] + cross_in[number]
    for quarter in range(4):
        for number in range(2):
            ref = returned(1 - mine, quarter * 4, number)
            pltpu.make_async_copy(ref, ref, c_recv.at[2 * quarter + number]).wait()
    for copy in sends:
        copy.wait_send()


def restore_kernel(margin_ref, ordered_ref, diag_in, coupling_ref, diag_ref, sems):
    diag_copy = pltpu.make_async_copy(diag_in, diag_ref, sems.at[2])
    diag_copy.start()
    for part in range(2):
        keys = [order(margin_ref[part, a]) for a in range(NOV)]
        for a in range(NOV):
            at = sum((keys[b] < keys[a]).astype(jnp.int32) for b in range(NOV) if b != a)
            pltpu.make_async_copy(
                ordered_ref.at[part, at],
                coupling_ref.at[part, pl.ds(a * BLOCK, BLOCK)],
                sems.at[part],
            ).start()
    for part in range(2):
        whole = coupling_ref.at[part]
        pltpu.make_async_copy(whole, whole, sems.at[part]).wait()
    diag_copy.wait()


def body(parent, margin, counts, factor, local_inverse):
    sub, live, flipped, alive, local = gathered(parent, margin, counts, factor, local_inverse)
    vmem = pl.BlockSpec(memory_space=pltpu.VMEM)
    dma = pltpu.SemaphoreType.DMA
    ordered, diag = pl.pallas_call(
        update_kernel,
        out_shape=(
            jax.ShapeDtypeStruct((2, NOV, BLOCK, 256), jnp.bfloat16),
            jax.ShapeDtypeStruct((2, 2, BLOCK, BLOCK), jnp.float32),
        ),
        in_specs=[vmem] * 5,
        out_specs=(vmem, vmem),
        scratch_shapes=[
            pltpu.VMEM((2, NOV, BLOCK, BLOCK), jnp.bfloat16),
            pltpu.VMEM((2, BLOCK, BLOCK), jnp.float32),
            pltpu.VMEM((2, BLOCK, BLOCK), jnp.float32),
            dma((8,)), dma((8,)), dma((2,)), dma((2,)),
        ],
        compiler_params=pltpu.CompilerParams(
            collective_id=1, has_side_effects=True, vmem_limit_bytes=24 * 2**20
        ),
        cost_estimate=pl.CostEstimate(
            flops=6 * 10**9, bytes_accessed=20 * 2**20, transcendentals=0
        ),
    )(sub.reshape(BLOCKS, BLOCK, BLOCK), live, flipped, alive, local)
    hbm = pl.BlockSpec(memory_space=pl.ANY)
    return pl.pallas_call(
        restore_kernel,
        out_shape=(
            jax.ShapeDtypeStruct(factor.shape, jnp.bfloat16),
            jax.ShapeDtypeStruct((2, 2, BLOCK, BLOCK), jnp.float32),
        ),
        in_specs=[pl.BlockSpec(memory_space=pltpu.SMEM), vmem, vmem],
        out_specs=(hbm, hbm),
        scratch_shapes=[dma((3,))],
        compiler_params=pltpu.CompilerParams(vmem_limit_bytes=8 * 2**20),
    )(margin, ordered, diag)


def solution(mesh):
    placed = (
        P(("front", "row"), None),
        P("front", None),
        P("front"),
        P("front", None, "row"),
        P("front", None, "row"),
    )
    return jax.shard_map(
        body,
        mesh=mesh,
        in_specs=placed,
        out_specs=(P("front", None, "row"), P("front", "row", None, None)),
        check_vma=False,
    )
```
